32 devices in a mesh: section: 2 (over core), dp: 4 (over z), ns: 4 (over y, x).
Axes of the slice: x: 2, y: 2, z: 4, core: 2. Of those that a mesh axis runs over, the one named last changes fastest.
Arguments:
- inputs: bfloat16 [32, 1024, 512], P(('dp', 'ns')), may hold values from -6 to 6
- cotangent: bfloat16 [32, 1024, 512], P(('dp', 'ns')), may hold values from -6 to 6
- lengths: int32 [32], P(('dp', 'ns')), may hold values from 256 to 1024, as said below
- species: int32 [32], P(('dp', 'ns')), may hold values from 0 to 7
- conv_weight: float32 [2, 4608, 512], P('section', 'ns'), may hold values from -0.09375 to 0.09375
- up_weight: float32 [2, 512, 2048], P('section', None, 'ns'), may hold values from -0.25 to 0.25
- down_weight: float32 [2, 2048, 512], P('section', 'ns'), may hold values from -0.125 to 0.125
- conv_moment: float32 [2, 4608, 512], P('section', 'ns')
- up_moment: float32 [2, 512, 2048], P('section', None, 'ns')
- down_moment: float32 [2, 2048, 512], P('section', 'ns')
- vec_values: float32 [2, 10, 512], P('section')
- vec_first: float32 [2, 10, 512], P('section')
- vec_second: float32 [2, 10, 512], P('section')
- head_weight: bfloat16 [512, 6], replicated, may hold values from -0.375 to 0.375
- head_bias: float32 [6], replicated, may hold values from -4 to 4
Outputs:
- activations: bfloat16 [2, 32, 1024, 512], P('section', ('dp', 'ns'))
- input_grad: bfloat16 [2, 32, 1024, 512], P('section', ('dp', 'ns'))
- conv_grad: float32 [2, 4608, 512], P('section', 'ns')
- up_grad: float32 [2, 512, 2048], P('section', None, 'ns')
- down_grad: float32 [2, 2048, 512], P('section', 'ns')
- conv_momentum: float32 [2, 4608, 512], P('section', 'ns')
- up_momentum: float32 [2, 512, 2048], P('section', None, 'ns')
- down_momentum: float32 [2, 2048, 512], P('section', 'ns')
- conv_new: float32 [2, 4608, 512], P('section', 'ns')
- up_new: float32 [2, 512, 2048], P('section', None, 'ns')
- down_new: float32 [2, 2048, 512], P('section', 'ns')
- conv_copy: bfloat16 [2, 4608, 512], P('section', 'ns')
- up_copy: bfloat16 [2, 512, 2048], P('section', None, 'ns')
- down_copy: bfloat16 [2, 2048, 512], P('section', 'ns')
- vec_grad: float32 [2, 10, 512], P('section')
- vec_first_new: float32 [2, 10, 512], P('section')
- vec_second_new: float32 [2, 10, 512], P('section')
- vec_new: float32 [2, 10, 512], P('section')
- species_freq: float32 [2, 8, 6], P('section')
- species_share: float32 [2, 8], P('section')
The draws below stay inside these ranges and needn't reach their ends.
Inputs may be any that keep to these rules, and one draw needn't show every extreme that they name: `lengths`: each length is 256, 512 or 1024; the first window has 256 and the last 1024.
All inputs are finite; a program needn't handle non-finite values.
Results may differ from the reference program's by a relative error of at most 0.011.
Values may be sent and summed in bfloat16 or wider, within the bound.
No kernel may reach another device: no remote copies, remote signals or barrier semaphores. Data moves between devices by JAX's collectives and lax.ppermute only.
A program may use at most 320 MiB of HBM per device.

```python
import math
import jax
import jax.numpy as jnp
from jax import lax

D = 512
FF = 2048
WIN = 1024
SECOND_DILATION = 32
MB = 2
SPECIES = 8
STEP = 10
WINDOWS = 32
GROUPS = 4


def gradient_scale():
    return 0.6 * math.sqrt(WINDOWS * WIN)


def ramp_along(shape, axis):
    extent = shape[axis]
    ramp = jnp.arange(extent, dtype=jnp.float32) / max(extent - 1, 1)
    view = [1] * len(shape)
    view[axis] = extent
    return ramp.reshape(view)


def draw_lengths(key, part):
    key = jax.random.fold_in(key, 5)
    window = jnp.arange(WINDOWS)
    device = window // MB
    lanes = WINDOWS // (MB * GROUPS)
    data_rank = device // GROUPS
    row_rank = device % GROUPS
    score = data_rank * max(GROUPS - 1, 1) + row_rank * max(lanes - 1, 1)
    span = 2 * max(lanes - 1, 1) * max(GROUPS - 1, 1)
    offset = jax.random.randint(key, (WINDOWS,), 0, span + 1)
    level = 3 * (offset + score) // (2 * span + 1)
    level = jnp.minimum(level, 2)
    length = jnp.where(level == 0, WIN // 4, jnp.where(level == 1, WIN // 2, WIN))
    length = length.at[0].set(WIN // 4).at[WINDOWS - 1].set(WIN)
    return length.astype(jnp.int32)


def draw_conv_moment(key, part):
    key = jax.random.fold_in(key, 11)
    shape = (2, 9 * D, D)
    ramp = ramp_along(shape, 1)
    values = jnp.clip(jax.random.normal(key, shape, jnp.float32), -4.0, 4.0) * (0.5 + 2.5 * ramp)
    return values * gradient_scale()


def draw_up_moment(key, part):
    key = jax.random.fold_in(key, 12)
    shape = (2, D, FF)
    ramp = ramp_along(shape, 2)
    values = jnp.clip(jax.random.normal(key, shape, jnp.float32), -4.0, 4.0) * (0.5 + 2.5 * ramp)
    return values * gradient_scale()


def draw_down_moment(key, part):
    key = jax.random.fold_in(key, 13)
    shape = (2, FF, D)
    ramp = ramp_along(shape, 1)
    values = jnp.clip(jax.random.normal(key, shape, jnp.float32), -4.0, 4.0) * (0.5 + 2.5 * ramp)
    return values * gradient_scale()


def draw_vec_values(key, part):
    key = jax.random.fold_in(key, 21)
    shape = (2, 10, D)
    rows = jnp.arange(10)[None, :, None]
    is_gain = (rows == 1) | (rows == 8)
    noise = jnp.clip(jax.random.normal(key, shape, jnp.float32), -4.0, 4.0)
    return jnp.where(is_gain, 1.0 + 0.1 * noise, 0.5 * noise)


def draw_vec_first(key, part):
    key = jax.random.fold_in(key, 22)
    shape = (2, 10, D)
    noise = jnp.clip(jax.random.normal(key, shape, jnp.float32), -4.0, 4.0)
    return 0.11 * gradient_scale() * noise


def draw_vec_second(key, part):
    key = jax.random.fold_in(key, 23)
    shape = (2, 10, D)
    factor = jnp.exp(jax.random.uniform(key, shape, jnp.float32, 0.0, math.log(4.0)))
    scale = gradient_scale()
    return 0.0526 * scale * scale * factor


def with_ends(result, stream_key, smallest, largest):
    shape = result.shape
    place = [jax.random.randint(jax.random.fold_in(stream_key, axis), (), 0, shape[axis]) for axis in range(len(shape))]
    result = result.at[tuple(place)].set(smallest)
    longest = shape.index(max(shape))
    place[longest] = (place[longest] + 1) % shape[longest]
    return result.at[tuple(place)].set(largest)


def block_levels(rng, dims, split, smallest, largest):
    loudness = 1.0
    for position, blocks in split:
        draws = jax.random.uniform(jax.random.fold_in(jax.random.fold_in(rng, 6), position), (blocks,), jnp.float32, smallest / len(split), largest / len(split))
        loudness = loudness * jnp.repeat(jnp.exp(draws), dims[position] // blocks).reshape((-1,) + (1,) * (len(dims) - 1 - position))
    return loudness


def normal_values(rng, dims, width, limit, cuts=(), kind=jnp.bfloat16):
    array = jax.random.normal(rng, dims, jnp.float32) * width
    if len(cuts) > 0:
        array = block_levels(rng, dims, cuts, -0.22, 0.18) * array
    return jnp.clip(array, min=-limit, max=limit).astype(kind)


def setup_inputs(seed: int = 0) -> dict:
    splits = jax.random.split(jax.random.key(seed), 16)
    inputs = normal_values(splits[0], (WINDOWS, WIN, D), 1.0, 6.0, ((0, 16),))
    cotangent = normal_values(splits[1], (WINDOWS, WIN, D), 1.0, 6.0, ((0, 16),))
    lengths = draw_lengths(jax.random.fold_in(splits[15], 71), 0)
    species = with_ends(jax.random.randint(splits[3], (WINDOWS,), 0, SPECIES), jax.random.fold_in(splits[3], 1), 0, SPECIES - 1).astype(jnp.int32)
    conv_weight = normal_values(splits[4], (2, 9 * D, D), (9 * D) ** -0.5, 0.09375, ((0, 2), (1, 4)), jnp.float32)
    up_weight = normal_values(splits[5], (2, D, FF), D ** -0.5, 0.25, ((0, 2), (2, 4)), jnp.float32)
    down_weight = normal_values(splits[6], (2, FF, D), FF ** -0.5, 0.125, ((0, 2), (1, 4)), jnp.float32)
    conv_moment = draw_conv_moment(jax.random.fold_in(splits[15], 71), 0)
    up_moment = draw_up_moment(jax.random.fold_in(splits[15], 71), 0)
    down_moment = draw_down_moment(jax.random.fold_in(splits[15], 71), 0)
    vec_values = draw_vec_values(jax.random.fold_in(splits[15], 71), 0)
    vec_first = draw_vec_first(jax.random.fold_in(splits[15], 71), 0)
    vec_second = draw_vec_second(jax.random.fold_in(splits[15], 71), 0)
    head_weight = normal_values(splits[13], (D, 6), (D // 2) ** -0.5, 0.375)
    head_bias = normal_values(splits[14], (6,), 1.0, 4.0, (), jnp.float32)
    return dict(inputs=inputs, cotangent=cotangent, lengths=lengths, species=species, conv_weight=conv_weight, up_weight=up_weight, down_weight=down_weight, conv_moment=conv_moment, up_moment=up_moment, down_moment=down_moment, vec_values=vec_values, vec_first=vec_first, vec_second=vec_second, head_weight=head_weight, head_bias=head_bias)


@jax.custom_vjp
def low(v):
    return lax.optimization_barrier(v.astype(jnp.bfloat16)).astype(jnp.float32)

@jax.custom_vjp
def low_back(v):
    return v

def low_keep(v):
    return (low(v), None)

def low_pass(kept, grad):
    return (grad,)

def back_keep(v):
    return (v, None)

def back_low(kept, grad):
    return (low(grad),)
low.defvjp(low_keep, low_pass)
low_back.defvjp(back_keep, back_low)
PRECISE = lax.Precision.HIGHEST
NORM_EPSILON = 1e-05
GRAM_EPSILON = 1e-07
ADAM_EPSILON = 1e-08
SCHULZ_LINEAR = 3.4445
SCHULZ_CUBIC = -4.775
SCHULZ_QUINTIC = 2.0315
MUON_MOMENTUM = 0.5
MUON_RATE = 0.1
MUON_DECAY = 0.01
ADAM_RATE = 0.5
ADAM_DECAY = 0.01
BETA_ONE = 0.9
BETA_TWO = 0.95

def layer_norm(feature_maps, gain_vec, bias_vec):
    average = lax.optimization_barrier(jnp.mean(feature_maps, axis=-1, keepdims=True))
    centred = feature_maps - average
    variance = lax.optimization_barrier(jnp.mean(centred * centred, axis=-1, keepdims=True))
    return centred * lax.rsqrt(variance + NORM_EPSILON) * gain_vec + bias_vec

def spread_taps(masked, tap_spacing):
    edge_margin = 4 * tap_spacing
    padded = jnp.pad(masked, ((0, 0), (edge_margin, edge_margin), (0, 0)))
    pieces = [padded[:, edge_margin + (tap_index - 4) * tap_spacing:edge_margin + (tap_index - 4) * tap_spacing + WIN, :] for tap_index in range(9)]
    return jnp.concatenate(pieces, axis=-1)

def residual_conv_block(values_in, padding_mask, weight_tensors, tap_spacing):
    conv_matrix, up_matrix, down_matrix, vectors = weight_tensors
    values_in = low_back(values_in)
    masked = values_in * padding_mask[..., None]
    stacked = spread_taps(masked, tap_spacing)
    conv_out = low_back(jnp.einsum('bti,io->bto', stacked, low(conv_matrix), precision=PRECISE) + vectors[0])
    middle = values_in + layer_norm(jax.nn.gelu(conv_out), vectors[1], vectors[2])
    hidden_pre = low_back(jnp.einsum('bti,if->btf', low(middle), low(up_matrix), precision=PRECISE) + vectors[3:7].reshape(FF))
    hidden = low(jax.nn.gelu(hidden_pre))
    branch_out = low_back(jnp.einsum('btf,fo->bto', hidden, low(down_matrix), precision=PRECISE) + vectors[7])
    return middle + layer_norm(branch_out, vectors[8], vectors[9])

def orthogonalize(moment):
    matrix = moment * lax.rsqrt(jnp.sum(moment * moment) + GRAM_EPSILON)
    for sweep_index in range(5):
        gram_mat = jnp.dot(matrix.T, matrix, precision=PRECISE, preferred_element_type=jnp.float32)
        polynomial = SCHULZ_CUBIC * gram_mat + SCHULZ_QUINTIC * jnp.dot(gram_mat, gram_mat, precision=PRECISE, preferred_element_type=jnp.float32)
        matrix = SCHULZ_LINEAR * matrix + jnp.dot(matrix, polynomial, precision=PRECISE, preferred_element_type=jnp.float32)
    return matrix

def reference(inputs, cotangent, lengths, species, conv_weight, up_weight, down_weight, conv_moment, up_moment, down_moment, vec_values, vec_first, vec_second, head_weight, head_bias):
    params = [(conv_weight[section_id], up_weight[section_id], down_weight[section_id], vec_values[section_id]) for section_id in range(2)]
    group_size = math.gcd(WINDOWS, 4)
    group_count = WINDOWS // group_size
    head_matrix = head_weight.astype(jnp.float32)
    head_shift = head_bias.astype(jnp.float32)
    species_range = jnp.arange(SPECIES)
    positions = jnp.arange(WIN)

    def scan_step(running, slices):
        gradients, prob_sums, token_counts = running
        values_in, cotangent_in, window_len, species_ids = slices
        padding_mask = (positions[None, :] < window_len[:, None]).astype(jnp.float32)

        def section_one(feature_maps, weight_tensors):
            return low(residual_conv_block(feature_maps, padding_mask, weight_tensors, 1))

        def section_two(feature_maps, weight_tensors):
            return residual_conv_block(feature_maps, padding_mask, weight_tensors, SECOND_DILATION)
        first_out, pull_one = jax.vjp(section_one, values_in.astype(jnp.float32), params[0])
        second_out, pull_two = jax.vjp(section_two, first_out, params[1])
        first_grad, grads_two = pull_two(cotangent_in.astype(jnp.float32) * padding_mask[..., None])
        input_grad, grads_one = pull_one(first_grad)
        gradients = jax.tree.map(jnp.add, gradients, (grads_one, grads_two))
        second_low = low(second_out)
        species_hit = (species_ids[:, None] == species_range[None, :]).astype(jnp.float32)
        section_sums = []
        for block_out in (first_out, second_low):
            logits = jnp.einsum('btd,dc->btc', block_out, head_matrix, precision=PRECISE) + head_shift
            chances = jax.nn.softmax(logits, axis=-1)
            weighted = lax.optimization_barrier(jnp.sum(chances * padding_mask[..., None], axis=1))
            section_sums.append(jnp.einsum('gs,gc->sc', species_hit, weighted, precision=PRECISE))
        prob_sums = prob_sums + jnp.stack(section_sums)
        token_counts = token_counts + jnp.einsum('gs,g->s', species_hit, lax.optimization_barrier(jnp.sum(padding_mask, axis=1)), precision=PRECISE)
        return ((gradients, prob_sums, token_counts), (first_out, second_low, input_grad, first_grad))
    zero_grads = (jax.tree.map(jnp.zeros_like, params[0]), jax.tree.map(jnp.zeros_like, params[1]))
    start = (zero_grads, jnp.zeros((2, SPECIES, 6), jnp.float32), jnp.zeros((SPECIES,), jnp.float32))
    slices = (inputs.reshape(group_count, group_size, WIN, D), cotangent.reshape(group_count, group_size, WIN, D), lengths.reshape(group_count, group_size), species.reshape(group_count, group_size))
    (gradients, prob_sums, token_counts), stacked_out = lax.scan(scan_step, start, slices)
    first_out, second_out, input_first, input_second = [part.reshape(WINDOWS, WIN, D) for part in stacked_out]
    activations = jnp.stack([first_out, second_out]).astype(jnp.bfloat16)
    input_grad = jnp.stack([input_first, input_second]).astype(jnp.bfloat16)
    results = [[] for listing in range(18)]
    for section_id in range(2):
        grad_conv, grad_up, grad_down, grad_vec = gradients[section_id]
        conv_state = MUON_MOMENTUM * conv_moment[section_id] + grad_conv
        up_state = MUON_MOMENTUM * up_moment[section_id] + grad_up
        down_state = MUON_MOMENTUM * down_moment[section_id] + grad_down
        keep = 1.0 - MUON_RATE * MUON_DECAY
        conv_next = conv_weight[section_id] * keep - MUON_RATE * 0.2 * math.sqrt(9 * D) * orthogonalize(conv_state)
        up_next = up_weight[section_id] * keep - MUON_RATE * 0.2 * math.sqrt(FF) * orthogonalize(up_state.T).T
        down_next = down_weight[section_id] * keep - MUON_RATE * 0.2 * math.sqrt(FF) * orthogonalize(down_state)
        first_next = BETA_ONE * vec_first[section_id] + (1.0 - BETA_ONE) * grad_vec
        second_next = BETA_TWO * vec_second[section_id] + (1.0 - BETA_TWO) * grad_vec * grad_vec
        vec_next = vec_values[section_id] * (1.0 - ADAM_RATE * ADAM_DECAY) - ADAM_RATE * (first_next / (1.0 - BETA_ONE ** STEP)) / (jnp.sqrt(second_next / (1.0 - BETA_TWO ** STEP)) + ADAM_EPSILON)
        entries = [grad_conv, grad_up, grad_down, conv_state, up_state, down_state, conv_next, up_next, down_next, conv_next.astype(jnp.bfloat16), up_next.astype(jnp.bfloat16), down_next.astype(jnp.bfloat16), grad_vec, first_next, second_next, vec_next, prob_sums[section_id] / jnp.maximum(token_counts, 1.0)[:, None], SPECIES * token_counts / jnp.sum(token_counts)]
        for slot, entry in enumerate(entries):
            results[slot].append(entry)
    stacked = [jnp.stack(entry_list) for entry_list in results]
    return (activations, input_grad, stacked[0], stacked[1], stacked[2], stacked[3], stacked[4], stacked[5], stacked[6], stacked[7], stacked[8], stacked[9], stacked[10], stacked[11], stacked[12], stacked[13], stacked[14], stacked[15], stacked[16], stacked[17])
```

```python
import math

import jax
import jax.numpy as jnp
from jax import lax
from jax.sharding import PartitionSpec as P

D = 512
FF = 2048
SECOND_DILATION = 32
SPECIES = 8
STEP = 10


PRECISE = lax.Precision.HIGHEST
NORM_EPSILON = 1e-05
GRAM_EPSILON = 1e-07
ADAM_EPSILON = 1e-08
SCHULZ_LINEAR = 3.4445
SCHULZ_CUBIC = -4.775
SCHULZ_QUINTIC = 2.0315
MUON_MOMENTUM = 0.5
MUON_RATE = 0.1
MUON_DECAY = 0.01
ADAM_RATE = 0.5
ADAM_DECAY = 0.01
BETA_ONE = 0.9
BETA_TWO = 0.95

SWAP = [(0, 1), (1, 0)]


def swap_cores(value):
    return lax.ppermute(value, "section", SWAP)


def flip_bit(value, axis, bit):
    count = lax.axis_size(axis)
    return lax.ppermute(value, axis, [(source, source ^ bit) for source in range(count)])


def bits_of(axis):
    return [1 << power for power in range(int(math.log2(lax.axis_size(axis))))]


def turned(bits, part):
    start = part * len(bits) // 2
    return bits[start:] + bits[:start]


def at(array, index, axis=0):
    return lax.dynamic_index_in_dim(array, index, axis, keepdims=False)


def in_order(core, mine, other, axis=0):
    first = jnp.where(core == 0, mine, other)
    second = jnp.where(core == 0, other, mine)
    return jnp.stack([first, second], axis=axis)


def gather_rows(piece, axis):
    count = lax.axis_size(axis)
    me = lax.axis_index(axis)
    rows = piece.shape[0]
    half = rows // 2
    parts = []
    for part, first in enumerate((0, half)):
        held = {0: lax.slice_in_dim(piece, first, first + half)}
        for bit in turned(bits_of(axis), part):
            keys = sorted(held)
            got = flip_bit(jnp.stack([held[key] for key in keys]), axis, bit)
            for place, key in enumerate(keys):
                held[key ^ bit] = got[place]
        parts.append(held)
    whole = jnp.zeros((count, rows) + piece.shape[1:], piece.dtype)
    for part, first in enumerate((0, half)):
        for key, value in parts[part].items():
            whole = lax.dynamic_update_slice(
                whole, value[None], (me ^ key, first) + (0,) * (piece.ndim - 1)
            )
    return whole


def scatter_sum(chunks, axis):
    me = lax.axis_index(axis)
    count, rows = chunks.shape[:2]
    half = rows // 2
    sums = []
    for part, first in enumerate((0, half)):
        held = {
            key: lax.slice_in_dim(at(chunks, me ^ key), first, first + half)
            for key in range(count)
        }
        for bit in turned(bits_of(axis), part):
            keep = [key for key in sorted(held) if not key & bit]
            sent = jnp.stack([held[key ^ bit].astype(jnp.bfloat16) for key in keep])
            got = flip_bit(sent, axis, bit)
            held = {
                key: held[key] + got[place].astype(jnp.float32) for place, key in enumerate(keep)
            }
        sums.append(held[0])
    return jnp.concatenate(sums)


def sum_along(value, axis):
    me = lax.axis_index(axis)
    count = lax.axis_size(axis)
    rows = value.shape[0] // count
    parts = value.reshape((count, rows) + value.shape[1:])
    total = at(parts, me)
    low = parts.astype(jnp.bfloat16)
    for step in range(1, count):
        moves = [(source, (source + step) % count) for source in range(count)]
        total = total + lax.ppermute(at(low, (me + step) % count), axis, moves).astype(jnp.float32)
    total = total.astype(jnp.bfloat16)
    whole = jnp.zeros((count,) + total.shape, total.dtype)
    whole = lax.dynamic_update_index_in_dim(whole, total, me, 0)
    for step in range(1, count):
        moves = [(source, (source + step) % count) for source in range(count)]
        got = lax.ppermute(total, axis, moves)
        whole = lax.dynamic_update_index_in_dim(whole, got, (me - step) % count, 0)
    return whole.reshape(value.shape)


def sum_whole(value, axes):
    for axis in axes:
        for bit in bits_of(axis):
            value = value + flip_bit(value, axis, bit)
    return value


def sum_halves(value, axis):
    half = value.shape[0] // 2
    halves = []
    for part, first in enumerate((0, half)):
        piece = lax.slice_in_dim(value, first, first + half)
        for bit in turned(bits_of(axis), part):
            piece = piece + flip_bit(piece, axis, bit)
        halves.append(piece)
    return jnp.concatenate(halves)


def gather_weights(core, shard):
    rows = shard.shape[0] // 2
    halves = shard.reshape((2, rows) + shard.shape[1:])
    mine = at(halves, core)
    got = swap_cores(at(halves, 1 - core))
    whole = []
    for block in range(2):
        half = jnp.where(core == block, mine, got)
        full = gather_rows(half, "ns")
        other = swap_cores(full)
        whole.append(in_order(core, full, other, axis=1))
    return whole


def reduce_grad(core, chunks):
    count, rows = chunks.shape[:2]
    halves = chunks.reshape((count, 2, rows // 2) + chunks.shape[2:])
    sent = at(halves, 1 - core, 1).astype(jnp.bfloat16)
    both = at(halves, core, 1) + swap_cores(sent).astype(jnp.float32)
    return sum_along(scatter_sum(both, "ns"), "dp")


def schulz(gram):
    scale = lax.rsqrt(jnp.trace(gram) + GRAM_EPSILON)
    mul = lambda left, right: jnp.dot(
        left, right, precision=PRECISE, preferred_element_type=jnp.float32
    )
    eye = jnp.eye(gram.shape[0], dtype=jnp.float32)
    gram = gram * (scale * scale)
    turn = None
    for sweep_index in range(5):
        square = mul(gram, gram)
        poly = SCHULZ_LINEAR * eye + SCHULZ_CUBIC * gram + SCHULZ_QUINTIC * square
        turn = poly if turn is None else mul(turn, poly)
        if sweep_index < 4:
            gram = mul(gram, mul(poly, poly))
    return turn * scale


def layer_norm(feature_maps, gain_vec, bias_vec):
    average = jnp.mean(feature_maps, axis=-1, keepdims=True)
    centred = feature_maps - average
    variance = jnp.mean(centred * centred, axis=-1, keepdims=True)
    return centred * lax.rsqrt(variance + NORM_EPSILON) * gain_vec + bias_vec


def first_piece(conv_out, values_in, gain_vec, bias_vec):
    return values_in + layer_norm(jax.nn.gelu(conv_out), gain_vec, bias_vec)


def second_piece(branch_out, middle, gain_vec, bias_vec):
    return middle + layer_norm(branch_out, gain_vec, bias_vec)


def spread_taps(masked, tap_spacing):
    win_len = masked.shape[0]
    edge_margin = 4 * SECOND_DILATION
    padded = jnp.pad(masked, ((edge_margin, edge_margin), (0, 0)))
    pieces = [
        lax.slice_in_dim(padded, edge_margin + (tap_index - 4) * tap_spacing, edge_margin + (tap_index - 4) * tap_spacing + win_len)
        for tap_index in range(9)
    ]
    return jnp.concatenate(pieces, axis=1)


def collect_taps(spread_grad, tap_spacing):
    win_len = spread_grad.shape[0]
    feature = spread_grad.shape[1] // 9
    edge_margin = 4 * SECOND_DILATION
    summed = jnp.zeros((win_len, feature), jnp.float32)
    for tap_index in range(9):
        column_block = jnp.pad(
            spread_grad[:, tap_index * feature : (tap_index + 1) * feature],
            ((edge_margin, edge_margin), (0, 0)),
        )
        first = edge_margin - (tap_index - 4) * tap_spacing
        summed = summed + lax.slice_in_dim(column_block, first, first + win_len)
    return summed


def contract_rows(left, right):
    return lax.dot_general(
        left, right, (((0,), (0,)), ((), ())), preferred_element_type=jnp.float32
    )


def contract_cols(left, right):
    return lax.dot_general(
        left, right, (((1,), (1,)), ((), ())), preferred_element_type=jnp.float32
    )


def tall_gram(matrix):
    return lax.dot_general(
        matrix,
        matrix,
        (((0,), (0,)), ((), ())),
        precision=PRECISE,
        preferred_element_type=jnp.float32,
    )


def wide_gram(matrix):
    return lax.dot_general(
        matrix,
        matrix,
        (((1,), (1,)), ((), ())),
        precision=PRECISE,
        preferred_element_type=jnp.float32,
    )


def forward(block_input, padding_mask, tap_spacing, matrices, vectors):
    conv_full, up_full, down_full = matrices
    masked = block_input * padding_mask[:, None].astype(jnp.bfloat16)
    stacked = spread_taps(masked, tap_spacing)
    conv_out = jnp.dot(stacked, conv_full, preferred_element_type=jnp.float32) + vectors[0]
    middle = first_piece(conv_out, block_input.astype(jnp.float32), vectors[1], vectors[2])
    middle_low = middle.astype(jnp.bfloat16)
    hidden_pre = jnp.dot(middle_low, up_full, preferred_element_type=jnp.float32) + vectors[
        3:7
    ].reshape(-1)
    hidden = jax.nn.gelu(hidden_pre).astype(jnp.bfloat16)
    branch_out = jnp.dot(hidden, down_full, preferred_element_type=jnp.float32) + vectors[7]
    block_out = second_piece(branch_out, middle, vectors[8], vectors[9]).astype(jnp.bfloat16)
    return (block_out, (stacked, conv_out, middle, middle_low, hidden_pre, hidden, branch_out))


def backward(context, grad_out, block_input, padding_mask, tap_spacing, matrices, vectors):
    conv_full, up_full, down_full = matrices
    stacked, conv_out, middle, middle_low, hidden_pre, hidden, branch_out = context
    feature = vectors.shape[1]
    unused, pull_two = jax.vjp(second_piece, branch_out, middle, vectors[8], vectors[9])
    d_out, d_middle_res, d_gain_two, d_shift_two = pull_two(grad_out)
    d_out_low = d_out.astype(jnp.bfloat16)
    g_down = contract_rows(hidden, d_out_low)
    d_hidden = contract_cols(d_out_low, down_full)
    unused_pre, pull_gelu = jax.vjp(jax.nn.gelu, hidden_pre)
    (d_pre,) = pull_gelu(d_hidden)
    d_pre_low = d_pre.astype(jnp.bfloat16)
    g_up = contract_rows(middle_low, d_pre_low)
    d_middle = d_middle_res + contract_cols(d_pre_low, up_full)
    unused_conv, pull_one = jax.vjp(
        first_piece, conv_out, block_input.astype(jnp.float32), vectors[1], vectors[2]
    )
    d_conv, d_input_res, d_gain_one, d_shift_one = pull_one(d_middle)
    d_conv_low = d_conv.astype(jnp.bfloat16)
    g_conv = contract_rows(stacked, d_conv_low)
    d_stacked = contract_cols(d_conv_low, conv_full)
    d_input = d_input_res + collect_taps(d_stacked, tap_spacing) * padding_mask[:, None]
    g_vec = jnp.concatenate(
        [
            jnp.sum(d_conv_low, axis=0, dtype=jnp.float32)[None],
            d_gain_one[None],
            d_shift_one[None],
            jnp.sum(d_pre_low, axis=0, dtype=jnp.float32).reshape(4, feature),
            jnp.sum(d_out_low, axis=0, dtype=jnp.float32)[None],
            d_gain_two[None],
            d_shift_two[None],
        ],
        axis=0,
    )
    return (d_input.astype(jnp.bfloat16), (g_conv, g_up, g_down, g_vec))


def on_device(
    inputs,
    cotangent,
    lengths,
    species,
    conv_weight,
    up_weight,
    down_weight,
    conv_moment,
    up_moment,
    down_moment,
    vec_values,
    vec_first,
    vec_second,
    head_weight,
    head_bias,
):
    core = lax.axis_index("section")
    groups = lax.axis_size("ns")
    feature = inputs.shape[2]
    conv_low = conv_weight[0].astype(jnp.bfloat16)
    pair_low = jnp.concatenate(
        [
            up_weight[0].astype(jnp.bfloat16).reshape(-1, feature),
            down_weight[0].astype(jnp.bfloat16),
        ]
    )
    up_rows = up_weight[0].size // feature
    conv_full = gather_weights(core, conv_low)
    pair_full = gather_weights(core, pair_low)
    vectors = in_order(core, vec_values[0], swap_cores(vec_values[0]))
    matrices = []
    for block in range(2):
        pair = pair_full[block].reshape(groups, -1, feature)
        up_parts = pair[:, :up_rows].reshape(groups, feature, -1)
        matrices.append(
            (
                conv_full[block].reshape(-1, feature),
                up_parts.transpose(1, 0, 2).reshape(feature, -1),
                pair[:, up_rows:].reshape(-1, feature),
            )
        )
    batches = inputs.shape[0] // 2
    win_len = inputs.shape[1]
    positions = jnp.arange(win_len)
    species_range = jnp.arange(SPECIES)
    prob_sums = [jnp.zeros((SPECIES, head_weight.shape[1]), jnp.float32)] * 2
    token_counts = jnp.zeros((SPECIES,), jnp.float32)
    gradients = [None, None]
    outputs = [[], []]
    input_grads = [[], []]
    for batch in range(batches):
        window = core * batches + batch
        padding_mask = (positions < at(lengths, window)).astype(jnp.float32)
        species_hit = (species_range == at(species, window)).astype(jnp.float32)
        token_counts = token_counts + species_hit * jnp.sum(padding_mask)
        values = at(inputs, window)
        contexts = []
        for block in range(2):
            block_in = values
            spacing = (1, SECOND_DILATION)[block]
            values, context = forward(
                block_in, padding_mask, spacing, matrices[block], vectors[block]
            )
            logits = jnp.dot(values, head_weight, preferred_element_type=jnp.float32) + head_bias
            chances = jax.nn.softmax(logits, axis=-1)
            weighted = jnp.sum(chances * padding_mask[:, None], axis=0)
            prob_sums[block] = prob_sums[block] + species_hit[:, None] * weighted[None, :]
            outputs[block].append(values)
            contexts.append((block_in, context))
        grad = at(cotangent, window).astype(jnp.float32) * padding_mask[:, None]
        for block in (1, 0):
            block_in, context = contexts[block]
            grad_low, terms = backward(
                context,
                grad,
                block_in,
                padding_mask,
                (1, SECOND_DILATION)[block],
                matrices[block],
                vectors[block],
            )
            input_grads[block].append(grad_low)
            grad = grad_low.astype(jnp.float32)
            if gradients[block] is None:
                gradients[block] = terms
            else:
                gradients[block] = tuple(a + b for a, b in zip(gradients[block], terms))

    def own_windows(parts):
        mine = jnp.stack(parts[0]), jnp.stack(parts[1])
        got = swap_cores(jnp.where(core == 0, mine[1], mine[0]))
        joined = in_order(core, jnp.where(core == 0, mine[0], mine[1]), got)
        return joined.reshape((1, 2 * batches) + joined.shape[2:])

    activations = own_windows(outputs)
    input_grad = own_windows(input_grads)

    reduced = []
    for block in (1, 0):
        g_conv, g_up, g_down, g_vec = gradients[block]
        up_parts = g_up.reshape(feature, groups, -1).transpose(1, 0, 2)
        pair = jnp.concatenate(
            [
                up_parts.reshape(groups, -1, feature),
                g_down.reshape(groups, -1, feature),
            ],
            axis=1,
        )
        conv = reduce_grad(core, g_conv.reshape(groups, -1, feature))
        pair = reduce_grad(core, pair)
        reduced.append((conv, pair))
    reduced.reverse()

    def own_rows(place):
        mine = jnp.where(core == 0, reduced[0][place], reduced[1][place])
        got = swap_cores(jnp.where(core == 0, reduced[1][place], reduced[0][place]))
        joined = in_order(core, mine, got)
        return joined.reshape((-1, feature)).astype(jnp.float32)

    conv_grad = own_rows(0)
    pair_grad = own_rows(1)
    up_grad = pair_grad[:up_rows].reshape(feature, -1)
    down_grad = pair_grad[up_rows:]
    conv_state = MUON_MOMENTUM * conv_moment[0] + conv_grad
    up_state = MUON_MOMENTUM * up_moment[0] + up_grad
    down_state = MUON_MOMENTUM * down_moment[0] + down_grad

    def small_parts(block):
        tail = jnp.concatenate([prob_sums[block].reshape(-1), token_counts])
        tail = jnp.pad(tail, (0, feature - tail.size))
        return jnp.concatenate([gradients[block][3], tail[None]])

    mine, theirs = small_parts(0), small_parts(1)
    small = jnp.where(core == 0, mine, theirs) + swap_cores(jnp.where(core == 0, theirs, mine))
    small = sum_whole(small, ("ns", "dp"))
    vec_grad = small[:-1]
    prob_total = small[-1, : prob_sums[0].size].reshape(prob_sums[0].shape)
    count_total = small[-1, prob_sums[0].size : prob_sums[0].size + SPECIES]

    conv_turn = schulz(sum_halves(tall_gram(conv_state), "ns"))
    up_turn = schulz(sum_halves(wide_gram(up_state), "ns"))
    down_turn = schulz(sum_halves(tall_gram(down_state), "ns"))
    conv_orth = jnp.dot(conv_state, conv_turn, precision=PRECISE)
    up_orth = jnp.dot(up_turn.T, up_state, precision=PRECISE)
    down_orth = jnp.dot(down_state, down_turn, precision=PRECISE)
    keep_factor = 1.0 - MUON_RATE * MUON_DECAY
    conv_next = conv_weight[0] * keep_factor - MUON_RATE * 0.2 * math.sqrt(9 * D) * conv_orth
    up_next = up_weight[0] * keep_factor - MUON_RATE * 0.2 * math.sqrt(FF) * up_orth
    down_next = down_weight[0] * keep_factor - MUON_RATE * 0.2 * math.sqrt(FF) * down_orth
    first_next = BETA_ONE * vec_first[0] + (1.0 - BETA_ONE) * vec_grad
    second_next = BETA_TWO * vec_second[0] + (1.0 - BETA_TWO) * vec_grad * vec_grad
    vec_next = vec_values[0] * (1.0 - ADAM_RATE * ADAM_DECAY) - ADAM_RATE * (
        first_next / (1.0 - BETA_ONE**STEP)
    ) / (jnp.sqrt(second_next / (1.0 - BETA_TWO**STEP)) + ADAM_EPSILON)
    species_freq = prob_total / jnp.maximum(count_total, 1.0)[:, None]
    species_share = SPECIES * count_total / jnp.sum(count_total)
    return (
        activations,
        input_grad,
        conv_grad[None],
        up_grad[None],
        down_grad[None],
        conv_state[None],
        up_state[None],
        down_state[None],
        conv_next[None],
        up_next[None],
        down_next[None],
        conv_next.astype(jnp.bfloat16)[None],
        up_next.astype(jnp.bfloat16)[None],
        down_next.astype(jnp.bfloat16)[None],
        vec_grad[None],
        first_next[None],
        second_next[None],
        vec_next[None],
        species_freq[None],
        species_share[None],
    )


def solution(mesh):
    placed = (
        P(("dp", "ns"), None, None),
        P(("dp", "ns"), None, None),
        P(("dp", "ns")),
        P(("dp", "ns")),
        P("section", "ns", None),
        P("section", None, "ns"),
        P("section", "ns", None),
        P("section", "ns", None),
        P("section", None, "ns"),
        P("section", "ns", None),
        P("section", None, None),
        P("section", None, None),
        P("section", None, None),
        P(),
        P(),
    )
    return jax.shard_map(
        on_device,
        mesh=mesh,
        in_specs=placed,
        out_specs=(
            P("section", ("dp", "ns"), None, None),
            P("section", ("dp", "ns"), None, None),
            P("section", "ns", None),
            P("section", None, "ns"),
            P("section", "ns", None),
            P("section", "ns", None),
            P("section", None, "ns"),
            P("section", "ns", None),
            P("section", "ns", None),
            P("section", None, "ns"),
            P("section", "ns", None),
            P("section", "ns", None),
            P("section", None, "ns"),
            P("section", "ns", None),
            P("section", None, None),
            P("section", None, None),
            P("section", None, None),
            P("section", None, None),
            P("section", None, None),
            P("section", None),
        ),
        check_vma=False,
    )
```

```python
import functools
import math

import jax
import jax.numpy as jnp
from jax import lax
from jax.experimental import pallas as pl
from jax.experimental.pallas import tpu as pltpu
from jax.sharding import PartitionSpec as P

D = 512
FF = 2048
SECOND_DILATION = 32
SPECIES = 8
STEP = 10
TAPS = 9


NORM_EPSILON = 1e-05
GRAM_EPSILON = 1e-07
ADAM_EPSILON = 1e-08
SCHULZ_LINEAR = 3.4445
SCHULZ_CUBIC = -4.775
SCHULZ_QUINTIC = 2.0315
MUON_MOMENTUM = 0.5
MUON_RATE = 0.1
MUON_DECAY = 0.01
ADAM_RATE = 0.5
ADAM_DECAY = 0.01
BETA_ONE = 0.9
BETA_TWO = 0.95

SPACINGS = (1, SECOND_DILATION)
SWAP = [(0, 1), (1, 0)]
LANES = 128
VMEM_BYTES = 56 * 1024 * 1024
GELU_SCALE = 0.7978845608028654
GELU_CUBE = 0.044715


def swap_cores(value):
    return lax.ppermute(value, "section", SWAP)


def flip_bit(value, axis, bit):
    count = lax.axis_size(axis)
    return lax.ppermute(value, axis, [(source, source ^ bit) for source in range(count)])


def bits_of(axis):
    return [1 << power for power in range(int(math.log2(lax.axis_size(axis))))]


def turned(bits, part):
    start = part * len(bits) // 2
    return bits[start:] + bits[:start]


def at(array, index, axis=0):
    return lax.dynamic_index_in_dim(array, index, axis, keepdims=False)


def in_order(core, mine, other, axis=0):
    first = jnp.where(core == 0, mine, other)
    second = jnp.where(core == 0, other, mine)
    return jnp.stack([first, second], axis=axis)


def together(values, *fences):
    return lax.optimization_barrier((list(values), fences))[0]


class Task:
    def __init__(self, steps):
        self.steps = steps
        self.result = None
        self.wanted = next(steps)

    def give(self, got):
        try:
            self.wanted = self.steps.send(got)
        except StopIteration as end:
            self.wanted, self.result = None, end.value


def run(tasks, work=None, also=()):
    tasks = [task for task in tasks if task.wanted]
    wanted = [move for task in tasks for move in task.wanted]
    leaving = together([array for array, _ in wanted])
    made = work(leaving) if work else []
    arrived = [move(array) for array, (_, move) in zip(leaving, wanted)]
    arrived = together(arrived, made, also)
    for task in tasks:
        count = len(task.wanted)
        task.give(arrived[:count])
        arrived = arrived[count:]
    return made


def finish(task, *others):
    while task.wanted:
        run([task, *others])
    return task.result


def flips(axis, bit):
    return functools.partial(flip_bit, axis=axis, bit=bit)


def gather_rows(whole, axis):
    half = whole.shape[0] // 2
    held = [{0: part} for part in jnp.split(whole, 2)]
    arrays, places, others = [whole[None]], [[(0, 0)]], []
    fresh = arrays
    bits = [turned(bits_of(axis), part) for part in range(2)]
    for stage in range(len(bits[0]) + 1):
        moves = [(array, swap_cores) for array in fresh]
        last = stage == len(bits[0])
        if not last:
            for part in range(2):
                sent = jnp.stack([held[part][key] for key in sorted(held[part])])
                moves.append((sent, flips(axis, bits[part][stage])))
        got = yield moves
        others += got[: len(fresh)]
        fresh = got[len(fresh) :]
        arrays = arrays + fresh
        if not last:
            for part, array in enumerate(fresh):
                keys = sorted(held[part])
                bit = bits[part][stage]
                places.append([(key ^ bit, part * half) for key in keys])
                for place, key in enumerate(keys):
                    held[part][key ^ bit] = array[place]
    return arrays, others, places


def sum_cores(own, keep, send):
    (got,) = yield [(send, swap_cores)]
    return add_cores(own, keep, got)


def reduce_groups(keep, send):
    (got,) = yield [(send, swap_cores)]
    axis = "ns"
    bits = [turned(bits_of(axis), part) for part in range(2)]
    halves = keep.shape[1] // 2
    terms = [[(keep, part * halves), (got, part * halves)] for part in range(2)]
    keys = [list(range(keep.shape[0])) for part in range(2)]
    for stage in range(len(bits[0])):
        now = [bits[part][stage] for part in range(2)]
        sent, kept = split_sums(terms, halves, now, keys)
        keys = [[key for key in keys[part] if not key & now[part]] for part in range(2)]
        got = yield [(sent[part], flips(axis, bits[part][stage])) for part in range(2)]
        terms = [[(kept[part], 0), (got[part], 0)] for part in range(2)]
    axis = "dp"
    count = lax.axis_size(axis)
    me = lax.axis_index(axis)
    mine, *sent = last_sums(me, terms, halves, count)

    def move(step):
        moves = [(source, (source + step) % count) for source in range(count)]
        return lambda array: lax.ppermute(array, axis, moves)

    got = yield [(array, move(step + 1)) for step, array in enumerate(sent)]
    total = add_all([mine] + got)
    got = yield [(total, move(step)) for step in range(1, count)]
    return [total] + got


def sum_both_ways(parts, axis):
    for stage in range(len(bits_of(axis))):
        got = yield [
            (value, flips(axis, turned(bits_of(axis), part)[stage]))
            for part, value in enumerate(parts)
        ]
        parts = [a + b for a, b in zip(parts, got)]
    return parts


def sum_small(value, other):
    (got,) = yield [(other, swap_cores)]
    value = value + got
    for axis in ("ns", "dp"):
        for bit in bits_of(axis):
            (got,) = yield [(value, flips(axis, bit))]
            value = value + got
    return value


def own_block(scalars, first, second):
    mine, other = join_parts(scalars, first, second)
    (got,) = yield [(other, swap_cores)]
    return mine, got


def dot(left, right, contract=((1,), (0,))):
    return lax.dot_general(left, right, (contract, ((), ())), preferred_element_type=jnp.float32)


def gelu_parts(v):
    square = v * v
    bend = jnp.tanh(v * (GELU_SCALE + GELU_SCALE * GELU_CUBE * square))
    return 0.5 * v * (1.0 + bend), bend, square


def gelu_slope(v, bend, square):
    inner = GELU_SCALE + 3.0 * GELU_SCALE * GELU_CUBE * square
    return 0.5 * (1.0 + bend) + 0.5 * v * (1.0 - bend * bend) * inner


def normed(v):
    centred = v - jnp.mean(v, axis=-1, keepdims=True)
    scale = lax.rsqrt(jnp.mean(centred * centred, axis=-1, keepdims=True) + NORM_EPSILON)
    return centred * scale, scale


def norm_back(e, n, scale):
    return scale * (
        e - jnp.mean(e, axis=-1, keepdims=True) - n * jnp.mean(e * n, axis=-1, keepdims=True)
    )


def row_mask(first, rows, length):
    place = first + lax.broadcasted_iota(jnp.int32, (rows, 1), 0)
    return (place < length).astype(jnp.float32)


def start_all(copies):
    for copy in copies:
        copy.start()
    for copy in copies:
        copy.wait()


def fetch(scalars, block, mine, other):
    @pl.when(scalars[2] == block)
    def _():
        for copy in mine:
            copy.start()

    @pl.when(scalars[2] != block)
    def _():
        for copy in other:
            copy.start()

    return mine


def conv_fetch(scalars, block, places, refs, weight, sem):
    sides = []
    for side in range(2):
        copies = []
        for index, blocks in enumerate(places):
            ref = refs[side * len(places) + index]
            rows = ref.shape[1]
            for inner, (key, first) in enumerate(blocks):
                row = (scalars[1] ^ key) * refs[0].shape[1] + first
                target = weight.at[pl.ds(pl.multiple_of(row, 16), rows), :]
                copies.append(pltpu.make_async_copy(ref.at[inner], target, sem))
        sides.append(copies)
    return fetch(scalars, block, *sides)


def pair_fetch(scalars, block, refs, weights, sem):
    sides = [[pltpu.make_async_copy(ref, weights, sem)] for ref in refs]
    return fetch(scalars, block, *sides)


def spread(scratch, values, spacing):
    margin = (scratch.shape[0] - values.shape[0]) // 2
    rows = values.shape[0]
    zeros = jnp.zeros((margin, values.shape[1]), scratch.dtype)
    scratch[pl.ds(0, margin), :] = zeros
    scratch[pl.ds(margin + rows, margin), :] = zeros
    scratch[pl.ds(margin, rows), :] = values.astype(scratch.dtype)


def conv_forward_kernel(spacing, block, places, scalars, x_ref, v_ref, *refs):
    count = 2 * len(places)
    n_ref, slope_ref, mid_ref, low_ref, weight, padded, sem = refs[count:]
    step = pl.program_id(0)
    rows = mid_ref.shape[0]
    margin = (padded.shape[0] - x_ref.shape[0]) // 2

    @pl.when(step == 0)
    def _():
        copies = conv_fetch(scalars, block, places, refs[:count], weight, sem)
        spread(
            padded,
            x_ref[...].astype(jnp.float32) * row_mask(0, x_ref.shape[0], scalars[0]),
            spacing,
        )
        for copy in copies:
            copy.wait()

    first = pl.multiple_of(step * rows, rows)
    total = jnp.zeros(mid_ref.shape, jnp.float32)
    for tap in range(TAPS):
        shift = margin + (tap - 4) * spacing
        if spacing % 16 == 0:
            piece = padded[pl.ds(pl.multiple_of(first + shift, 16), rows), :]
        else:
            piece = pltpu.roll(padded[pl.ds(first, rows + 2 * margin), :], rows + 2 * margin - shift, 0)
            piece = piece[:rows].astype(jnp.bfloat16)
        total = total + dot(piece, weight[pl.ds(tap * D, D), :])
    total = total + v_ref[0:1, :]
    active, bend, square = gelu_parts(total)
    n, scale = normed(active)
    n_ref[...] = n.astype(jnp.bfloat16)
    slope_ref[...] = (gelu_slope(total, bend, square) * scale).astype(jnp.bfloat16)
    middle = (
        x_ref[pl.ds(first, rows), :].astype(jnp.float32) + n * v_ref[1:2, :] + v_ref[2:3, :]
    )
    mid_ref[...] = middle
    low_ref[...] = middle.astype(jnp.bfloat16)


def pair_forward_kernel(block, scalars, mid_ref, v_ref, bias_ref, head_ref, head_bias_ref, *refs):
    slope_ref, hid_ref, n_ref, scale_ref, out_ref, prob_ref, weights, sem = refs[2:]
    step = pl.program_id(0)
    rows = mid_ref.shape[0]

    @pl.when(step == 0)
    def _():
        copies = pair_fetch(scalars, block, refs[:2], weights, sem)
        prob_ref[...] = jnp.zeros_like(prob_ref)
        for copy in copies:
            copy.wait()

    middle = mid_ref[...]
    low = middle.astype(jnp.bfloat16)
    groups, wide = weights.shape[0], weights.shape[3]
    total = jnp.zeros(middle.shape, jnp.float32)
    for group in range(groups):
        pre = dot(low, weights[group, 0]) + bias_ref[group : group + 1, :]
        hidden, bend, square = gelu_parts(pre)
        hidden = hidden.astype(jnp.bfloat16)
        hid_ref[:, pl.ds(group * wide, wide)] = hidden
        slope_ref[:, pl.ds(group * wide, wide)] = gelu_slope(pre, bend, square).astype(
            jnp.bfloat16
        )
        total = total + dot(hidden, weights[group, 1], ((1,), (1,)))
    total = total + v_ref[7:8, :]
    n, scale = normed(total)
    n_ref[...] = n.astype(jnp.bfloat16)
    scale_ref[...] = jnp.broadcast_to(scale, scale_ref.shape)
    out = (middle + n * v_ref[8:9, :] + v_ref[9:10, :]).astype(jnp.bfloat16)
    out_ref[...] = out
    logits = dot(out, head_ref[...]) + head_bias_ref[0:1, :]
    logits = logits - jnp.max(logits, axis=-1, keepdims=True)
    weights = jnp.exp(logits)
    chances = weights / jnp.sum(weights, axis=-1, keepdims=True)
    chances = chances * row_mask(step * rows, rows, scalars[0])
    prob_ref[...] += jnp.broadcast_to(jnp.sum(chances, axis=0, keepdims=True), prob_ref.shape)


def inner_backward_kernel(
    block,
    tiles,
    scalars,
    grad_ref,
    n2_ref,
    scale2_ref,
    slope2_ref,
    n1_ref,
    slope1_ref,
    v_ref,
    low_ref,
    hid_ref,
    *refs,
):
    dmid_ref, dconv_ref, sums_ref, bias_ref, keep_ref, send_ref = refs[2:8]
    weights, dpre, dout_t, low_t, sem = refs[8:]
    step = pl.program_id(0)
    rows = grad_ref.shape[0]
    groups, wide = weights.shape[0], weights.shape[3]

    def add_row(row, value):
        sums_ref[row : row + 1, :] += jnp.sum(value, axis=0, keepdims=True)

    @pl.when(step == 0)
    def _():
        copies = pair_fetch(scalars, block, refs[:2], weights, sem)
        sums_ref[...] = jnp.zeros_like(sums_ref)
        bias_ref[...] = jnp.zeros_like(bias_ref)
        low_t[...] = low_ref[...].T
        for copy in copies:
            copy.wait()

    @pl.when(step < tiles)
    def _():
        first = pl.multiple_of(step * rows, rows)
        grad = grad_ref[...].astype(jnp.float32) * row_mask(first, rows, scalars[0])
        n = n2_ref[...].astype(jnp.float32)
        add_row(8, grad * n)
        add_row(9, grad)
        d_out = norm_back(grad * v_ref[8:9, :], n, scale2_ref[:, 0:1]).astype(jnp.bfloat16)
        dout_t[:, pl.ds(first, rows)] = d_out.T
        add_row(7, d_out.astype(jnp.float32))
        d_middle = grad
        for group in range(groups):
            column = pl.ds(group * wide, wide)
            d_hidden = dot(d_out, weights[group, 1])
            d_pre = d_hidden * slope2_ref[:, column].astype(jnp.float32)
            bias_ref[group : group + 1, :] += jnp.sum(d_pre, axis=0, keepdims=True)
            d_pre = d_pre.astype(jnp.bfloat16)
            dpre[pl.ds(first, rows), column] = d_pre
            d_middle = d_middle + dot(d_pre, weights[group, 0], ((1,), (1,)))
        dmid_ref[...] = d_middle
        n = n1_ref[...].astype(jnp.float32)
        add_row(1, d_middle * n)
        add_row(2, d_middle)
        d_conv = norm_back(d_middle * v_ref[1:2, :], n, slope1_ref[...].astype(jnp.float32))
        dconv_ref[...] = d_conv.astype(jnp.bfloat16)
        add_row(0, d_conv)

    @pl.when(step >= tiles)
    def _():
        core = scalars[2]
        half = low_t.shape[0] // 2
        column = pl.ds(pl.multiple_of((step - tiles) * wide, wide), wide)
        for target, side in ((keep_ref, core), (send_ref, 1 - core)):
            place = pl.ds(pl.multiple_of(side * half, half), half)
            target[0, :half] = dot(low_t[place, :], dpre[:, column]).astype(jnp.bfloat16)
            target[0, half:] = dot(dout_t[place, :], hid_ref[...]).astype(jnp.bfloat16)


def conv_grad_kernel(spacing, block_index, places, scalars, x_ref, dconv_ref, dmid_hbm, *refs):
    count = 2 * len(places)
    keep_hbm, send_hbm, grad_ref = refs[count : count + 3]
    weight, padded, moved, xt, kept, sent, dmid, sems = refs[count + 3 :]
    own, core = scalars[1], scalars[2]
    rows = x_ref.shape[0]
    margin = (padded.shape[0] - rows) // 2
    chunk, wide = keep_hbm.shape[1:]
    block = math.gcd(chunk, D)
    weights = conv_fetch(scalars, block_index, places, refs[:count], weight, sems.at[0])
    residual = pltpu.make_async_copy(dmid_hbm, dmid, sems.at[1])
    residual.start()
    mask = row_mask(0, rows, scalars[0])
    xt[...] = (x_ref[...].astype(jnp.float32) * mask).astype(jnp.bfloat16).T
    spread(padded, dconv_ref[...].astype(jnp.float32), spacing)
    leaving = []
    for tap in range(TAPS):
        shift = margin - (tap - 4) * spacing
        if spacing % 16 == 0:
            shifted = padded[pl.ds(shift, rows), :]
        else:
            shifted = padded[pl.ds(shift, rows), :].astype(jnp.bfloat16)
            moved[tap] = shifted
        grad = dot(xt[...], shifted)
        left, right = grad[:, :wide].astype(jnp.bfloat16), grad[:, wide:].astype(jnp.bfloat16)
        kept[tap] = jnp.where(core == 0, left, right)
        sent[tap] = jnp.where(core == 0, right, left)
        for part in range(D // block):
            row = tap * D + part * block
            place = own ^ (row // chunk)
            for source, target in ((kept, keep_hbm), (sent, send_hbm)):
                copy = pltpu.make_async_copy(
                    source.at[tap, pl.ds(part * block, block), :],
                    target.at[place, pl.ds(row % chunk, block), :],
                    sems.at[2],
                )
                copy.start()
                leaving.append(copy)
    for copy in weights:
        copy.wait()
    total = jnp.zeros((rows, D), jnp.float32)
    for tap in range(TAPS):
        shift = margin - (tap - 4) * spacing
        shifted = padded[pl.ds(shift, rows), :] if spacing % 16 == 0 else moved[tap]
        total = total + dot(shifted, weight[pl.ds(tap * D, D), :], ((1,), (1,)))
    residual.wait()
    grad_ref[...] = (dmid[...] + mask * total).astype(jnp.bfloat16)
    for copy in leaving:
        copy.wait()


def split_low(value):
    high = value.astype(jnp.bfloat16)
    return high, (value - high.astype(jnp.float32)).astype(jnp.bfloat16)


def mul_same(left, right):
    half = left[0].shape[0] // 2

    def part(rows, columns):
        (a, b), (c, d) = [m[rows] for m in left], [m[:, columns] for m in right]
        return dot(a, c) + (dot(a, d) + dot(b, c))

    upper = part(slice(0, half), slice(None))
    corner = part(slice(half, None), slice(half, None))
    lower = jnp.concatenate([upper[:, half:].T, corner], axis=1)
    return jnp.concatenate([upper, lower], axis=0)


def tiles_of(rows):
    count = rows // LANES
    return [(i, j) for i in range(count) for j in range(i, count)]


def pack(gram, first_ref, second_ref):
    places = tiles_of(gram.shape[0])
    half = len(places) // 2
    for index, (i, j) in enumerate(places):
        tile_values = gram[i * LANES : (i + 1) * LANES, j * LANES : (j + 1) * LANES]
        ref, place = (first_ref, index) if index < half else (second_ref, index - half)
        ref[place] = tile_values


def unpack(first_ref, second_ref, rows):
    count = rows // LANES
    found = {}
    half = first_ref.shape[0]
    for index, (i, j) in enumerate(tiles_of(rows)):
        values = first_ref[index] if index < half else second_ref[index - half]
        found[i, j] = values
        if i != j:
            found[j, i] = values.T
    return jnp.concatenate(
        [jnp.concatenate([found[i, j] for j in range(count)], axis=1) for i in range(count)], axis=0
    )


def schulz_kernel(first_ref, second_ref, turn_ref):
    rows = turn_ref.shape[0]
    eye = (
        lax.broadcasted_iota(jnp.int32, (rows, rows), 0)
        == lax.broadcasted_iota(jnp.int32, (rows, rows), 1)
    ).astype(jnp.float32)
    raw = unpack(first_ref, second_ref, rows)
    trace = jnp.sum(jnp.sum(raw * eye, axis=0, keepdims=True), axis=1, keepdims=True)
    scale = lax.rsqrt(trace + GRAM_EPSILON)
    gram, turn = raw * (scale * scale), None
    for sweep in range(5):
        parts = split_low(gram)
        square = mul_same(parts, parts)
        poly = split_low(SCHULZ_LINEAR * eye + SCHULZ_CUBIC * gram + SCHULZ_QUINTIC * square)
        if sweep == 0:
            turn = poly
        elif sweep < 4:
            turn = split_low(mul_same(turn, poly))
        else:
            turn_ref[...] = mul_same(turn, poly) * scale
        if sweep < 4:
            gram = mul_same(parts, split_low(mul_same(poly, poly)))


def split_sums_kernel(bits, *refs):
    for part in range(2):
        (one, first_one), (two, first_two) = [
            (ref, first) for ref, first in zip(refs[2 * part : 2 * part + 2], bits[part][1])
        ]
        sent, kept = refs[4 + 2 * part : 6 + 2 * part]
        bit, rows = bits[part][0], sent.shape[1]
        counts = {False: 0, True: 0}
        for place, key in enumerate(bits[part][2]):
            leaves = bool(key & bit)
            value = one[place, pl.ds(first_one, rows), :].astype(jnp.float32) + two[
                place, pl.ds(first_two, rows), :
            ].astype(jnp.float32)
            (sent if leaves else kept)[counts[leaves]] = value.astype(jnp.bfloat16)
            counts[leaves] += 1


def last_sums_kernel(steps, scalars, *refs):
    *terms, total = refs[:4] + refs[-1:]
    targets = refs[4:-1]
    rows = terms[0].shape[1]
    for part in range(2):
        one, two = terms[2 * part : 2 * part + 2]
        total[pl.ds(part * rows, rows), :] = one[0].astype(jnp.float32) + two[0].astype(jnp.float32)
    share = targets[0].shape[0]
    for step, target in enumerate(targets):
        place = lax.rem(scalars[0] + step, steps)
        target[...] = total[pl.ds(pl.multiple_of(place * share, 8), share), :].astype(jnp.bfloat16)


def add_all_kernel(*refs):
    total = refs[0][...].astype(jnp.float32)
    for ref in refs[1:-1]:
        total = total + ref[...].astype(jnp.float32)
    refs[-1][...] = total.astype(jnp.bfloat16)


def add_cores_kernel(scalars, keep_ref, got_ref, out_ref):
    value = keep_ref[...].astype(jnp.float32) + got_ref[...].astype(jnp.float32)
    out_ref[...] = value.astype(jnp.bfloat16)


def join_parts_kernel(count, scalars, *refs):
    mine, other = refs[-2:]
    share = refs[0].shape[0]
    me, core = scalars[0], scalars[1]
    for step in range(count):
        place = pl.ds(pl.multiple_of(lax.rem(me + count - step, count) * share, 16), share)
        first, second = refs[step][...], refs[count][place, :]
        mine[place, :] = jnp.where(core == 0, first, second)
        other[place, :] = jnp.where(core == 0, second, first)


def conv_state_kernel(
    scalars, mine_ref, got_ref, moment_ref, grad_ref, state_ref, first_ref, second_ref, high, cross
):
    step = pl.program_id(0)
    mine, got = mine_ref[...].astype(jnp.float32), got_ref[...].astype(jnp.float32)
    core = scalars[0]
    grad = jnp.concatenate(
        [jnp.where(core == 0, mine, got), jnp.where(core == 0, got, mine)], axis=1
    )
    grad_ref[...] = grad
    state = MUON_MOMENTUM * moment_ref[...] + grad
    state_ref[...] = state
    top, low = split_low(state)

    @pl.when(step == 0)
    def _():
        high[...] = jnp.zeros_like(high)
        cross[...] = jnp.zeros_like(cross)

    high[...] += dot(top, top, ((0,), (0,)))
    cross[...] += dot(top, low, ((0,), (0,)))

    @pl.when(step == pl.num_programs(0) - 1)
    def _():
        mixed = cross[...]
        pack(high[...] + (mixed + mixed.T), first_ref, second_ref)


def pair_state_kernel(
    scalars,
    mine_ref,
    got_ref,
    up_moment_ref,
    down_moment_ref,
    up_grad_ref,
    down_grad_ref,
    up_state_ref,
    down_state_ref,
    *packed,
):
    core = scalars[0]
    mine, got = mine_ref[...].astype(jnp.float32), got_ref[...].astype(jnp.float32)
    left, right = jnp.where(core == 0, mine, got), jnp.where(core == 0, got, mine)
    half = mine.shape[0] // 2
    grads = [
        jnp.concatenate([left[place], right[place]], axis=0)
        for place in (slice(0, half), slice(half, None))
    ]
    up_grad_ref[...] = grads[0]
    down_grad = grads[1].T
    down_grad_ref[...] = down_grad
    up_state = MUON_MOMENTUM * up_moment_ref[...] + grads[0]
    up_state_ref[...] = up_state
    down_state = MUON_MOMENTUM * down_moment_ref[...] + down_grad
    down_state_ref[...] = down_state
    for state, contract, refs in (
        (up_state, ((1,), (1,)), packed[:2]),
        (down_state, ((0,), (0,)), packed[2:]),
    ):
        top, low = split_low(state)
        mixed = dot(top, low, contract)
        pack(dot(top, top, contract) + (mixed + mixed.T), *refs)


def params(**more):
    return pltpu.CompilerParams(vmem_limit_bytes=VMEM_BYTES, **more)


def cost(macs, moved=8 << 20):
    return pl.CostEstimate(flops=2 * macs, bytes_accessed=moved, transcendentals=0)


ANY = pl.BlockSpec(memory_space=pl.ANY)


def whole(shape):
    return pl.BlockSpec(shape, lambda *_: (0,) * len(shape))


def tile(rows, wide):
    return pl.BlockSpec((rows, wide), lambda step, *_: (step, 0))


def shape_of(shape, dtype):
    return jax.ShapeDtypeStruct(shape, dtype)


def call(kernel, grid, in_specs, out_specs, out_shape, scratch, macs, after=()):
    taken = 1 + len(in_specs)

    def body(*refs):
        kernel(*refs[:taken], *refs[taken + len(after) :])

    made = pl.pallas_call(
        body,
        grid_spec=pltpu.PrefetchScalarGridSpec(
            num_scalar_prefetch=1,
            grid=grid,
            in_specs=list(in_specs) + [ANY] * len(after),
            out_specs=out_specs,
            scratch_shapes=scratch,
        ),
        out_shape=out_shape,
        compiler_params=params(),
        cost_estimate=cost(macs),
    )
    return lambda *arrays: made(*arrays, *after)


def padded_scratch(win_len, spacing):
    margin = max(4 * spacing, 8)
    return pltpu.VMEM(
        (win_len + 2 * margin, D), jnp.bfloat16 if spacing % 16 == 0 else jnp.float32
    )


def conv_forward(scalars, x, vectors, gathered, block, after=()):
    spacing = SPACINGS[block]
    win_len = x.shape[0]
    rows = min(512, win_len)
    arrays, others, places = gathered
    arrays = arrays + others
    return call(
        functools.partial(conv_forward_kernel, spacing, block, places),
        (win_len // rows,),
        [whole(x.shape), whole(vectors.shape)] + [ANY] * len(arrays),
        [tile(rows, D)] * 4,
        [
            shape_of((win_len, D), jnp.bfloat16),
            shape_of((win_len, D), jnp.bfloat16),
            shape_of((win_len, D), jnp.float32),
            shape_of((win_len, D), jnp.bfloat16),
        ],
        [
            pltpu.VMEM((TAPS * D, D), jnp.bfloat16),
            padded_scratch(win_len, spacing),
            pltpu.SemaphoreType.DMA,
        ],
        win_len * TAPS * D * D,
        after,
    )(scalars, x, vectors, *arrays)


def pair_scratch(groups, wide):
    return [pltpu.VMEM((groups, 2, D, wide), jnp.bfloat16), pltpu.SemaphoreType.DMA]


def pair_forward(scalars, middle, vectors, bias, head, head_bias, pair, block, after=()):
    win_len = middle.shape[0]
    rows = min(512, win_len)
    groups, wide = bias.shape
    return call(
        functools.partial(pair_forward_kernel, block),
        (win_len // rows,),
        [
            tile(rows, D),
            whole(vectors.shape),
            whole(bias.shape),
            whole(head.shape),
            whole(head_bias.shape),
        ]
        + [ANY] * 2,
        [
            tile(rows, FF),
            tile(rows, FF),
            tile(rows, D),
            tile(rows, LANES),
            tile(rows, D),
            whole((8, LANES)),
        ],
        [
            shape_of((win_len, FF), jnp.bfloat16),
            shape_of((win_len, FF), jnp.bfloat16),
            shape_of((win_len, D), jnp.bfloat16),
            shape_of((win_len, LANES), jnp.float32),
            shape_of((win_len, D), jnp.bfloat16),
            shape_of((8, LANES), jnp.float32),
        ],
        pair_scratch(groups, wide),
        win_len * 2 * D * FF,
        after,
    )(scalars, middle, vectors, bias, head, head_bias, *pair)


def inner_backward(scalars, grad, saved, vectors, pair, block, groups, after=()):
    n1, slope1, low, slope2, hidden, n2, scale2 = saved
    win_len = grad.shape[0]
    rows = min(256, win_len)
    tiles = win_len // rows
    wide = FF // groups

    def early(columns):
        return pl.BlockSpec((rows, columns), lambda step, *_: (jnp.minimum(step, tiles - 1), 0))

    def group_of(step):
        return jnp.maximum(step - tiles, 0)

    column = pl.BlockSpec((win_len, wide), lambda step, *_: (0, group_of(step)))
    place = pl.BlockSpec((1, D, wide), lambda step, s: (group_of(step) ^ s[1], 0, 0))
    weights, sem = pair_scratch(groups, wide)
    return call(
        functools.partial(inner_backward_kernel, block, tiles),
        (tiles + groups,),
        [
            early(D),
            early(D),
            early(LANES),
            early(FF),
            early(D),
            early(D),
            whole(vectors.shape),
            whole(low.shape),
            column,
        ]
        + [ANY] * 2,
        [early(D), early(D), whole((16, D)), whole((groups, wide)), place, place],
        [
            shape_of((win_len, D), jnp.float32),
            shape_of((win_len, D), jnp.bfloat16),
            shape_of((16, D), jnp.float32),
            shape_of((groups, wide), jnp.float32),
            shape_of((groups, D, wide), jnp.bfloat16),
            shape_of((groups, D, wide), jnp.bfloat16),
        ],
        [
            weights,
            pltpu.VMEM((win_len, FF), jnp.bfloat16),
            pltpu.VMEM((D, win_len), jnp.bfloat16),
            pltpu.VMEM((D, win_len), jnp.bfloat16),
            sem,
        ],
        win_len * 4 * D * FF,
        after,
    )(scalars, grad, n2, scale2, slope2, n1, slope1, vectors, low, hidden, *pair)


def conv_grad(scalars, x, d_conv, d_middle, gathered, block, groups, after=()):
    win_len = x.shape[0]
    chunk = TAPS * D // groups
    spacing = SPACINGS[block]
    arrays, others, places = gathered
    arrays = arrays + others
    aligned = spacing % 16 == 0
    return call(
        functools.partial(conv_grad_kernel, spacing, block, places),
        (1,),
        [whole(x.shape), whole(x.shape), ANY] + [ANY] * len(arrays),
        [ANY, ANY, whole(x.shape)],
        [shape_of((groups, chunk, D // 2), jnp.bfloat16)] * 2
        + [shape_of((win_len, D), jnp.bfloat16)],
        [
            pltpu.VMEM((TAPS * D, D), jnp.bfloat16),
            padded_scratch(win_len, spacing),
            pltpu.VMEM((1, 16, LANES) if aligned else (TAPS, win_len, D), jnp.bfloat16),
            pltpu.VMEM((D, win_len), jnp.bfloat16),
            pltpu.VMEM((TAPS, D, D // 2), jnp.bfloat16),
            pltpu.VMEM((TAPS, D, D // 2), jnp.bfloat16),
            pltpu.VMEM((win_len, D), jnp.float32),
            pltpu.SemaphoreType.DMA((3,)),
        ],
        win_len * 2 * TAPS * D * D,
        after,
    )(scalars, x, d_conv, d_middle, *arrays)


def schulz(parts, after=()):
    def body(first_ref, second_ref, *refs):
        schulz_kernel(first_ref, second_ref, refs[-1])

    return pl.pallas_call(
        body,
        in_specs=[whole(part.shape) for part in parts] + [ANY] * len(after),
        out_specs=whole((D, D)),
        out_shape=shape_of((D, D), jnp.float32),
        compiler_params=params(),
        cost_estimate=cost(17 * 3 * D * D * D),
    )(*parts, *after)


def plain(kernel, arrays, out_shapes, scratch=(), scalars=None):
    if scalars is not None:
        return call(
            kernel,
            (1,),
            [whole(array.shape) for array in arrays],
            [whole(shape) for shape in out_shapes],
            [shape_of(shape, jnp.bfloat16) for shape in out_shapes],
            list(scratch),
            1 << 20,
        )(scalars, *arrays)
    return pl.pallas_call(
        kernel,
        out_shape=[shape_of(shape, jnp.bfloat16) for shape in out_shapes],
        compiler_params=params(),
        cost_estimate=cost(1 << 20),
    )(*arrays)


def split_sums(terms, rows, bits, keys):
    arrays = [array for part in terms for array, _ in part]
    plan = [
        (bit, [first for _, first in part], part_keys)
        for bit, part, part_keys in zip(bits, terms, keys)
    ]
    count, wide = arrays[0].shape[0], arrays[0].shape[2]
    outs = plain(
        functools.partial(split_sums_kernel, plan), arrays, [(count // 2, rows, wide)] * 4
    )
    return outs[0::2], outs[1::2]


def add_cores(own, keep, got):
    groups, rows, wide = keep.shape
    relative = pl.BlockSpec((1, rows, wide), lambda step, s: (step, 0, 0))
    return call(
        add_cores_kernel,
        (groups,),
        [relative, relative],
        pl.BlockSpec((1, rows, wide), lambda step, s: (step ^ s[0], 0, 0)),
        shape_of(keep.shape, jnp.bfloat16),
        [],
        1 << 20,
    )(own.reshape(1).astype(jnp.int32), keep, got)


def last_sums(me, terms, rows, count):
    arrays = [array for part in terms for array, _ in part]
    wide = arrays[0].shape[2]
    return plain(
        functools.partial(last_sums_kernel, count),
        arrays,
        [(2 * rows // count, wide)] * count,
        [pltpu.VMEM((2 * rows, wide), jnp.float32)],
        me.reshape(1).astype(jnp.int32),
    )


def add_all(arrays):
    return plain(add_all_kernel, arrays, [arrays[0].shape])[0]


def join_parts(scalars, first, second):
    count = len(first)
    share, wide = first[0].shape
    return plain(
        functools.partial(join_parts_kernel, count),
        [*first, second],
        [(count * share, wide)] * 2,
        (),
        scalars,
    )


def packed_shapes():
    count = len(tiles_of(D)) // 2
    return [(count, LANES, LANES)] * 2


def conv_states(core, mine, got, moment, after=()):
    chunk = moment.shape[0]
    rows = chunk // 3
    shapes = packed_shapes()
    return call(
        conv_state_kernel,
        (3,),
        [tile(rows, D // 2), tile(rows, D // 2), tile(rows, D)],
        [tile(rows, D), tile(rows, D)] + [whole(shape) for shape in shapes],
        [shape_of((chunk, D), jnp.float32)] * 2
        + [shape_of(shape, jnp.float32) for shape in shapes],
        [pltpu.VMEM((D, D), jnp.float32)] * 2,
        2 * chunk * D * D,
        after,
    )(core, mine, got, moment)


def pair_states(core, mine, got, up_moment, down_moment, after=()):
    shapes = packed_shapes() * 2
    outs = [up_moment.shape, down_moment.shape] * 2 + shapes
    return call(
        pair_state_kernel,
        (1,),
        [whole(value.shape) for value in (mine, got, up_moment, down_moment)],
        [whole(shape) for shape in outs],
        [shape_of(shape, jnp.float32) for shape in outs],
        [],
        4 * up_moment.shape[1] * D * D,
        after,
    )(core, mine, got, up_moment, down_moment)


def on_device(
    inputs,
    cotangent,
    lengths,
    species,
    conv_weight,
    up_weight,
    down_weight,
    conv_moment,
    up_moment,
    down_moment,
    vec_values,
    vec_first,
    vec_second,
    head_weight,
    head_bias,
):
    core = lax.axis_index("section")
    own = lax.axis_index("ns")
    groups = lax.axis_size("ns")
    feature = inputs.shape[2]
    wide = FF // groups

    pair = lax.all_gather(
        jnp.stack(
            [up_weight[0].astype(jnp.bfloat16), down_weight[0].astype(jnp.bfloat16).T]
        ),
        "ns",
    )
    conv = finish(Task(gather_rows(conv_weight[0].astype(jnp.bfloat16), "ns")))
    vectors = in_order(core, vec_values[0], swap_cores(vec_values[0]))
    (pair,) = together([pair], conv[1][-1])
    pair = (pair, swap_cores(pair))

    batches = inputs.shape[0] // 2
    win_len = inputs.shape[1]
    species_range = jnp.arange(SPECIES)
    classes = head_weight.shape[1]
    head = jnp.pad(head_weight, ((0, 0), (0, LANES - classes)))
    head_shift = jnp.pad(head_bias[None], ((0, 0), (0, LANES - classes)), constant_values=-1e30)
    prob_sums = [jnp.zeros((SPECIES, classes), jnp.float32)] * 2
    token_counts = jnp.zeros((SPECIES,), jnp.float32)
    kept = {}
    outputs = [[], []]
    input_grads = [[], []]

    def add_up(name, values):
        kept[name] = values if name not in kept else [a + b for a, b in zip(kept[name], values)]

    def own_windows(parts):
        mine = jnp.stack(parts[0]), jnp.stack(parts[1])
        (got,) = yield [(jnp.where(core == 0, mine[1], mine[0]), swap_cores)]
        joined = in_order(core, jnp.where(core == 0, mine[0], mine[1]), got)
        return joined.reshape((1, 2 * batches) + joined.shape[2:])

    for batch in range(batches):
        window = core * batches + batch
        length = at(lengths, window)
        scalars = jnp.stack([length, own, core]).astype(jnp.int32)
        species_hit = (species_range == at(species, window)).astype(jnp.float32)
        token_counts = token_counts + species_hit * length.astype(jnp.float32)
        values = at(inputs, window)
        last = batch == batches - 1
        contexts = []
        for block in range(2):
            x = values
            n1, slope1, middle, low = conv_forward(scalars, x, vectors[block], conv, block)
            bias = vectors[block][3:7].reshape(groups, wide)
            slope2, hidden, n2, scale2, values, probs = pair_forward(
                scalars,
                middle,
                vectors[block],
                bias,
                head,
                head_shift,
                pair,
                block,
            )
            prob_sums[block] = prob_sums[block] + species_hit[:, None] * probs[:1, :classes]
            outputs[block].append(values)
            contexts.append((x, (n1, slope1, low, slope2, hidden, n2, scale2)))
        grad = at(cotangent, window)
        last = batch == batches - 1
        for block in (1, 0):
            x, saved = contexts[block]

            def inner(after):
                return inner_backward(
                    scalars, grad, saved, vectors[block], pair, block, groups, after=after
                )

            def outer(after):
                return conv_grad(
                    scalars, x, d_conv, d_middle, conv, block, groups, after=after
                )

            if last and block == 0:
                conv_one = Task(sum_cores(own, *kept["conv", 1]))
                pair_one = lax.psum_scatter(pair_one.result, "ns", scatter_dimension=0)
                made = run([conv_one, shared_out], inner)
            else:
                made = inner(())
            d_middle, d_conv, sums, bias_sums, *pair_terms = made
            add_up(("pair", block), pair_terms)
            vec_sums = jnp.concatenate(
                [sums[0:3], bias_sums.reshape(-1, feature), sums[7:10]]
            )
            add_up(("vec", block), [vec_sums])
            if last and block == 1:
                pair_one = Task(sum_cores(own, *pair_terms))
                shared_out = Task(own_windows(outputs))
                *conv_terms, grad = run([pair_one], outer)
            elif last:
                pair_zero = Task(reduce_groups(*kept["pair", 0]))
                *conv_terms, grad = run([pair_zero], outer, also=[pair_one])
            else:
                *conv_terms, grad = outer(pair_terms)
            add_up(("conv", block), conv_terms)
            input_grads[block].append(grad)
    conv_zero = Task(reduce_groups(*kept["conv", 0]))
    conv_one = together([conv_one.result], pair_one)[0]
    conv_one = lax.psum_scatter(conv_one, "ns", scatter_dimension=0)

    def small_parts(block):
        tail = jnp.concatenate([prob_sums[block].reshape(-1), token_counts])
        tail = jnp.pad(tail, (0, feature - tail.size))
        return jnp.concatenate([kept["vec", block][0], tail[None]])

    mine, theirs = small_parts(0), small_parts(1)
    small = Task(
        sum_small(jnp.where(core == 0, mine, theirs), jnp.where(core == 0, theirs, mine))
    )
    shared_in = Task(own_windows(input_grads))
    run([pair_zero, conv_zero, small], also=[conv_one])
    conv_one, pair_one = lax.psum((conv_one, pair_one), "dp")
    while conv_zero.wanted:
        run([pair_zero, conv_zero, small])
    finish(pair_zero, conv_zero)
    finish(conv_zero)
    conv_one, pair_one = together([conv_one, pair_one], conv_zero.result)
    place = jnp.stack([lax.axis_index("dp"), core]).astype(jnp.int32)
    pair_all = Task(own_block(place, pair_zero.result, pair_one))
    conv_all = Task(own_block(place, conv_zero.result, conv_one))
    run([conv_all, pair_all, small, shared_in])
    core_scalar = core.reshape(1).astype(jnp.int32)
    conv_total, conv_state, *conv_gram = conv_states(
        core_scalar, *conv_all.result, conv_moment[0]
    )
    conv_gram = Task(sum_both_ways(conv_gram, "ns"))
    up_grad, down_grad, up_state, down_state, *grams = run(
        [conv_gram],
        lambda after: pair_states(
            core_scalar, *pair_all.result, up_moment[0], down_moment[0], after
        ),
    )
    up_gram = Task(sum_both_ways(grams[:2], "ns"))
    down_gram = Task(sum_both_ways(grams[2:], "ns"))
    run([conv_gram, up_gram])
    gram = finish(conv_gram)
    (conv_turn,) = run([up_gram, down_gram], lambda after: [schulz(gram, after)])
    gram = finish(up_gram)
    (up_turn,) = run([down_gram], lambda after: [schulz(gram, after)])
    down_turn = schulz(finish(down_gram))
    activations, input_grad, small = shared_out.result, shared_in.result, finish(small)
    vec_grad = small[:-1]
    prob_total = small[-1, : prob_sums[0].size].reshape(prob_sums[0].shape)
    count_total = small[-1, prob_sums[0].size : prob_sums[0].size + SPECIES]

    def product(left, right, contract):
        return lax.dot_general(
            left,
            right,
            (contract, ((), ())),
            precision=lax.Precision.HIGH,
            preferred_element_type=jnp.float32,
        )

    up_orth = product(up_turn, up_state, ((0,), (0,)))
    down_orth = product(down_state, down_turn, ((1,), (0,)))
    conv_orth = product(conv_state, conv_turn, ((1,), (0,)))
    keep_factor = 1.0 - MUON_RATE * MUON_DECAY
    conv_next = conv_weight[0] * keep_factor - MUON_RATE * 0.2 * math.sqrt(9 * D) * conv_orth
    up_next = up_weight[0] * keep_factor - MUON_RATE * 0.2 * math.sqrt(FF) * up_orth
    down_next = down_weight[0] * keep_factor - MUON_RATE * 0.2 * math.sqrt(FF) * down_orth
    first_next = BETA_ONE * vec_first[0] + (1.0 - BETA_ONE) * vec_grad
    second_next = BETA_TWO * vec_second[0] + (1.0 - BETA_TWO) * vec_grad * vec_grad
    vec_next = vec_values[0] * (1.0 - ADAM_RATE * ADAM_DECAY) - ADAM_RATE * (
        first_next / (1.0 - BETA_ONE**STEP)
    ) / (jnp.sqrt(second_next / (1.0 - BETA_TWO**STEP)) + ADAM_EPSILON)
    species_freq = prob_total / jnp.maximum(count_total, 1.0)[:, None]
    species_share = SPECIES * count_total / jnp.sum(count_total)
    return (
        activations,
        input_grad,
        conv_total[None],
        up_grad[None],
        down_grad[None],
        conv_state[None],
        up_state[None],
        down_state[None],
        conv_next[None],
        up_next[None],
        down_next[None],
        conv_next.astype(jnp.bfloat16)[None],
        up_next.astype(jnp.bfloat16)[None],
        down_next.astype(jnp.bfloat16)[None],
        vec_grad[None],
        first_next[None],
        second_next[None],
        vec_next[None],
        species_freq[None],
        species_share[None],
    )


def solution(mesh):
    placed = (
        P(("dp", "ns"), None, None),
        P(("dp", "ns"), None, None),
        P(("dp", "ns")),
        P(("dp", "ns")),
        P("section", "ns", None),
        P("section", None, "ns"),
        P("section", "ns", None),
        P("section", "ns", None),
        P("section", None, "ns"),
        P("section", "ns", None),
        P("section", None, None),
        P("section", None, None),
        P("section", None, None),
        P(),
        P(),
    )
    return jax.shard_map(
        on_device,
        mesh=mesh,
        in_specs=placed,
        out_specs=(
            P("section", ("dp", "ns"), None, None),
            P("section", ("dp", "ns"), None, None),
            P("section", "ns", None),
            P("section", None, "ns"),
            P("section", "ns", None),
            P("section", "ns", None),
            P("section", None, "ns"),
            P("section", "ns", None),
            P("section", "ns", None),
            P("section", None, "ns"),
            P("section", "ns", None),
            P("section", "ns", None),
            P("section", None, "ns"),
            P("section", "ns", None),
            P("section", None, None),
            P("section", None, None),
            P("section", None, None),
            P("section", None, None),
            P("section", None, None),
            P("section", None),
        ),
        check_vma=False,
    )
```

```python
import functools
import math

import jax
import jax.numpy as jnp
from jax import lax
from jax.experimental import pallas as pl
from jax.experimental.pallas import tpu as pltpu
from jax.sharding import PartitionSpec as P

D = 512
FF = 2048
SECOND_DILATION = 32
SPECIES = 8
STEP = 10
TAPS = 9


NORM_EPSILON = 1e-05
GRAM_EPSILON = 1e-07
ADAM_EPSILON = 1e-08
SCHULZ_LINEAR = 3.4445
SCHULZ_CUBIC = -4.775
SCHULZ_QUINTIC = 2.0315
MUON_MOMENTUM = 0.5
MUON_RATE = 0.1
MUON_DECAY = 0.01
ADAM_RATE = 0.5
ADAM_DECAY = 0.01
BETA_ONE = 0.9
BETA_TWO = 0.95

SPACINGS = (1, SECOND_DILATION)
SWAP = [(0, 1), (1, 0)]
LANES = 128
VMEM_BYTES = 56 * 1024 * 1024
LESS_BYTES = 24 * 1024 * 1024
GELU_SCALE = 0.7978845608028654
GELU_CUBE = 0.044715


def swap_cores(value):
    return lax.ppermute(value, "section", SWAP)


def flip_bit(value, axis, bit):
    count = lax.axis_size(axis)
    return lax.ppermute(value, axis, [(source, source ^ bit) for source in range(count)])


def bits_of(axis):
    return [1 << power for power in range(int(math.log2(lax.axis_size(axis))))]


def turned(bits, part):
    start = part * len(bits) // 2
    return bits[start:] + bits[:start]


def at(array, index, axis=0):
    return lax.dynamic_index_in_dim(array, index, axis, keepdims=False)


def in_order(core, mine, other, axis=0):
    first = jnp.where(core == 0, mine, other)
    second = jnp.where(core == 0, other, mine)
    return jnp.stack([first, second], axis=axis)


def together(values, *fences):
    return lax.optimization_barrier((list(values), fences))[0]


class Task:
    def __init__(self, steps):
        self.steps = steps
        self.result = None
        self.wanted = next(steps)

    def give(self, got):
        try:
            self.wanted = self.steps.send(got)
        except StopIteration as end:
            self.wanted, self.result = None, end.value


def run(tasks, work=None, also=()):
    tasks = [task for task in tasks if task.wanted]
    wanted = [move for task in tasks for move in task.wanted]
    leaving = together([array for array, _ in wanted])
    made = work(leaving) if work else []
    arrived = [move(array) for array, (_, move) in zip(leaving, wanted)]
    arrived = together(arrived, made, also)
    for task in tasks:
        count = len(task.wanted)
        task.give(arrived[:count])
        arrived = arrived[count:]
    return made


def finish(task, *others):
    while task.wanted:
        run([task, *others])
    return task.result


def flips(axis, bit):
    return functools.partial(flip_bit, axis=axis, bit=bit)


def gather_rows(part, axis):
    half = part.shape[0] // 2
    held = [{0: rows} for rows in jnp.split(part, 2)]
    arrays, places, others = [part[None]], [[(0, 0)]], []
    fresh = arrays
    bits = [turned(bits_of(axis), part) for part in range(2)]
    for stage in range(len(bits[0]) + 1):
        moves = []
        last = stage == len(bits[0])
        if not last:
            for side in range(2):
                sent = jnp.stack([held[side][key] for key in sorted(held[side])])
                moves.append((sent, flips(axis, bits[side][stage])))
        moves += [(array, swap_cores) for array in fresh]
        got = yield moves
        others += got[len(got) - len(fresh) :]
        fresh = got[: len(got) - len(fresh)]
        arrays = arrays + fresh
        if not last:
            for side, array in enumerate(fresh):
                keys = sorted(held[side])
                bit = bits[side][stage]
                places.append([(key ^ bit, side * half) for key in keys])
                for place, key in enumerate(keys):
                    held[side][key ^ bit] = array[place]
    return arrays, others, places


def sum_cores(own, keep, send):
    (got,) = yield [(send, swap_cores)]
    return add_cores(own, keep, got)


def reduce_groups(keep, send):
    (got,) = yield [(send, swap_cores)]
    axis = "ns"
    bits = [turned(bits_of(axis), part) for part in range(2)]
    halves = keep.shape[1] // 2
    terms = [[(keep, part * halves), (got, part * halves)] for part in range(2)]
    keys = [list(range(keep.shape[0])) for part in range(2)]
    for stage in range(len(bits[0])):
        now = [bits[part][stage] for part in range(2)]
        sent, kept = split_sums(terms, halves, now, keys)
        keys = [[key for key in keys[part] if not key & now[part]] for part in range(2)]
        got = yield [(sent[part], flips(axis, bits[part][stage])) for part in range(2)]
        terms = [[(kept[part], 0), (got[part], 0)] for part in range(2)]
    axis = "dp"
    count = lax.axis_size(axis)
    me = lax.axis_index(axis)
    mine, *sent = last_sums(me, terms, halves, count)

    def move(step):
        moves = [(source, (source + step) % count) for source in range(count)]
        return lambda array: lax.ppermute(array, axis, moves)

    got = yield [(array, move(step + 1)) for step, array in enumerate(sent)]
    total = add_all([mine] + got)
    got = yield [(total, move(step)) for step in range(1, count)]
    return [total] + got


def sum_both_ways(parts, axis):
    for stage in range(len(bits_of(axis))):
        if stage:
            parts = [a + b for a, b in terms]
        got = yield [
            (value, flips(axis, turned(bits_of(axis), part)[stage]))
            for part, value in enumerate(parts)
        ]
        terms = list(zip(parts, got))
    return terms


def sum_small(value, other):
    (got,) = yield [(other, swap_cores)]
    value = value + got
    for axis in ("ns", "dp"):
        for bit in bits_of(axis):
            (got,) = yield [(value, flips(axis, bit))]
            value = value + got
    return value


def own_block(mine, other):
    (got,) = yield [(other, swap_cores)]
    return mine, got


def dot(left, right, contract=((1,), (0,))):
    return lax.dot_general(left, right, (contract, ((), ())), preferred_element_type=jnp.float32)


def gelu_parts(v):
    square = v * v
    bend = jnp.tanh(v * (GELU_SCALE + GELU_SCALE * GELU_CUBE * square))
    return 0.5 * v * (1.0 + bend), bend, square


def gelu_slope(v, bend, square):
    inner = GELU_SCALE + 3.0 * GELU_SCALE * GELU_CUBE * square
    return 0.5 * (1.0 + bend) + 0.5 * v * (1.0 - bend * bend) * inner


def normed(v):
    centred = v - jnp.mean(v, axis=-1, keepdims=True)
    scale = lax.rsqrt(jnp.mean(centred * centred, axis=-1, keepdims=True) + NORM_EPSILON)
    return centred * scale, scale


def norm_back(e, n, scale):
    return scale * (
        e - jnp.mean(e, axis=-1, keepdims=True) - n * jnp.mean(e * n, axis=-1, keepdims=True)
    )


def row_mask(first, rows, length):
    place = first + lax.broadcasted_iota(jnp.int32, (rows, 1), 0)
    return (place < length).astype(jnp.float32)


def start_all(copies):
    for copy in copies:
        copy.start()
    for copy in copies:
        copy.wait()


def conv_copies(scalars, places, refs, weight, sem):
    copies = []
    for side in range(2):
        for index, blocks in enumerate(places):
            ref = refs[side * len(places) + index]
            rows, wide = ref.shape[1:]
            column = (scalars[2] if side == 0 else 1 - scalars[2]) * wide
            for inner, (key, first) in enumerate(blocks):
                row = (scalars[1] ^ key) * refs[0].shape[1] + first
                target = weight.at[
                    pl.ds(pl.multiple_of(row, 16), rows),
                    pl.ds(pl.multiple_of(column, LANES), wide),
                ]
                copies.append(pltpu.make_async_copy(ref.at[inner], target, sem))
    for copy in copies:
        copy.start()
    return copies


def pair_copies(scalars, block, refs, weights, sem):
    copies = []
    for side, ref in enumerate(refs):
        rows = ref.shape[3]
        row = (scalars[2] if side == 0 else 1 - scalars[2]) * rows
        target = weights.at[:, :, pl.ds(pl.multiple_of(row, 16), rows), :]
        copies.append(pltpu.make_async_copy(ref.at[:, block], target, sem))
    for copy in copies:
        copy.start()
    return copies


def spread(scratch, values, spacing):
    margin = (scratch.shape[0] - values.shape[0]) // 2
    rows = values.shape[0]
    zeros = jnp.zeros((margin, values.shape[1]), scratch.dtype)
    scratch[pl.ds(0, margin), :] = zeros
    scratch[pl.ds(margin + rows, margin), :] = zeros
    scratch[pl.ds(margin, rows), :] = values.astype(scratch.dtype)


def conv_forward_kernel(spacing, places, scalars, x_ref, v_ref, *refs):
    count = 2 * len(places)
    n_ref, slope_ref, mid_ref, low_ref, weight, padded, sem = refs[count:]
    step = pl.program_id(0)
    rows = mid_ref.shape[0]
    margin = (padded.shape[0] - x_ref.shape[0]) // 2

    @pl.when(step == 0)
    def _():
        copies = conv_copies(scalars, places, refs[:count], weight, sem)
        spread(
            padded,
            x_ref[...].astype(jnp.float32) * row_mask(0, x_ref.shape[0], scalars[0]),
            spacing,
        )
        for copy in copies:
            copy.wait()

    first = pl.multiple_of(step * rows, rows)
    total = jnp.zeros(mid_ref.shape, jnp.float32)
    for tap in range(TAPS):
        shift = margin + (tap - 4) * spacing
        if spacing % 16 == 0:
            piece = padded[pl.ds(pl.multiple_of(first + shift, 16), rows), :]
        else:
            piece = pltpu.roll(padded[pl.ds(first, rows + 2 * margin), :], rows + 2 * margin - shift, 0)
            piece = piece[:rows].astype(jnp.bfloat16)
        total = total + dot(piece, weight[pl.ds(tap * D, D), :])
    total = total + v_ref[0:1, :]
    active, bend, square = gelu_parts(total)
    n, scale = normed(active)
    n_ref[...] = n.astype(jnp.bfloat16)
    slope_ref[...] = (gelu_slope(total, bend, square) * scale).astype(jnp.bfloat16)
    middle = (
        x_ref[pl.ds(first, rows), :].astype(jnp.float32) + n * v_ref[1:2, :] + v_ref[2:3, :]
    )
    mid_ref[...] = middle
    low_ref[...] = middle.astype(jnp.bfloat16)


def feed_forward_end(scalars, first, total, middle, v_ref, head_ref, head_bias_ref, prob_ref):
    n, scale = normed(total + v_ref[7:8, :])
    out = (middle + n * v_ref[8:9, :] + v_ref[9:10, :]).astype(jnp.bfloat16)
    logits = dot(out, head_ref[...]) + head_bias_ref[0:1, :]
    logits = logits - jnp.max(logits, axis=-1, keepdims=True)
    weights = jnp.exp(logits)
    chances = weights / jnp.sum(weights, axis=-1, keepdims=True)
    chances = chances * row_mask(first, middle.shape[0], scalars[0])
    prob_ref[...] += jnp.broadcast_to(jnp.sum(chances, axis=0, keepdims=True), prob_ref.shape)
    return n, scale, out


def pair_forward_kernel(
    block, scalars, mid_ref, v_ref, bias_ref, head_ref, head_bias_ref, own_ref, other_ref, *refs
):
    n_ref, scale_ref, out_ref, prob_ref, weights, sem = refs
    step = pl.program_id(0)
    rows = mid_ref.shape[0]

    @pl.when(step == 0)
    def _():
        copies = pair_copies(scalars, block, (own_ref, other_ref), weights, sem)
        prob_ref[...] = jnp.zeros_like(prob_ref)
        for copy in copies:
            copy.wait()

    middle = mid_ref[...]
    low = middle.astype(jnp.bfloat16)
    total = jnp.zeros(middle.shape, jnp.float32)
    for group in range(weights.shape[0]):
        pre = dot(low, weights[group, 0]) + bias_ref[group : group + 1, :]
        hidden = gelu_parts(pre)[0].astype(jnp.bfloat16)
        total = total + dot(hidden, weights[group, 1], ((1,), (1,)))
    n, scale, out = feed_forward_end(
        scalars, step * rows, total, middle, v_ref, head_ref, head_bias_ref, prob_ref
    )
    n_ref[...] = n.astype(jnp.bfloat16)
    scale_ref[...] = jnp.broadcast_to(scale, scale_ref.shape)
    out_ref[...] = out


def inner_backward_kernel(block, tiles, forward, scalars, *refs):
    grad_ref, n1_ref, slope1_ref, v_ref, bias_ref, *refs = refs
    if forward:
        mid_ref, head_ref, head_bias_ref, *refs = refs
    else:
        low_ref, n2_ref, scale2_ref, *refs = refs
    own_ref, other_ref, *refs = refs
    dmid_ref, dconv_ref, sums_ref, bias_sums_ref, keep_ref, send_ref, *refs = refs
    if forward:
        out_ref, prob_ref, *refs = refs
    weights, slopes, hidden_all, dpre, dout_t, low_t, sem = refs
    step = pl.program_id(0)
    rows = grad_ref.shape[0]
    groups, wide = weights.shape[0], weights.shape[3]

    def add_row(row, value):
        sums_ref[row : row + 1, :] += jnp.sum(value, axis=0, keepdims=True)

    @pl.when(step == 0)
    def _():
        copies = pair_copies(scalars, block, (own_ref, other_ref), weights, sem)
        sums_ref[...] = jnp.zeros_like(sums_ref)
        bias_sums_ref[...] = jnp.zeros_like(bias_sums_ref)
        if forward:
            prob_ref[...] = jnp.zeros_like(prob_ref)
        for copy in copies:
            copy.wait()

    @pl.when(step < tiles)
    def _():
        first = pl.multiple_of(step * rows, rows)
        place = pl.ds(first, rows)
        low = mid_ref[...].astype(jnp.bfloat16) if forward else low_ref[...]
        low_t[:, place] = low.T
        total = jnp.zeros((rows, D), jnp.float32)
        for group in range(groups):
            column = pl.ds(group * wide, wide)
            pre = dot(low, weights[group, 0]) + bias_ref[group : group + 1, :]
            hidden, bend, square = gelu_parts(pre)
            hidden = hidden.astype(jnp.bfloat16)
            hidden_all[place, column] = hidden
            slopes[:, column] = gelu_slope(pre, bend, square).astype(jnp.bfloat16)
            if forward:
                total = total + dot(hidden, weights[group, 1], ((1,), (1,)))
        if forward:
            n, scale, out = feed_forward_end(
                scalars, first, total, mid_ref[...], v_ref, head_ref, head_bias_ref, prob_ref
            )
            out_ref[...] = out
        else:
            n, scale = n2_ref[...].astype(jnp.float32), scale2_ref[:, 0:1]
        grad = grad_ref[...].astype(jnp.float32) * row_mask(first, rows, scalars[0])
        add_row(8, grad * n)
        add_row(9, grad)
        d_out = norm_back(grad * v_ref[8:9, :], n, scale).astype(jnp.bfloat16)
        dout_t[:, place] = d_out.T
        add_row(7, d_out.astype(jnp.float32))
        d_middle = grad
        for group in range(groups):
            column = pl.ds(group * wide, wide)
            d_hidden = dot(d_out, weights[group, 1])
            d_pre = d_hidden * slopes[:, column].astype(jnp.float32)
            bias_sums_ref[group : group + 1, :] += jnp.sum(d_pre, axis=0, keepdims=True)
            d_pre = d_pre.astype(jnp.bfloat16)
            dpre[place, column] = d_pre
            d_middle = d_middle + dot(d_pre, weights[group, 0], ((1,), (1,)))
        dmid_ref[...] = d_middle
        n = n1_ref[...].astype(jnp.float32)
        add_row(1, d_middle * n)
        add_row(2, d_middle)
        d_conv = norm_back(d_middle * v_ref[1:2, :], n, slope1_ref[...].astype(jnp.float32))
        dconv_ref[...] = d_conv.astype(jnp.bfloat16)
        add_row(0, d_conv)

    @pl.when(step >= tiles)
    def _():
        core = scalars[2]
        half = low_t.shape[0] // 2
        column = pl.ds(pl.multiple_of((step - tiles) * wide, wide), wide)
        for target, side in ((keep_ref, core), (send_ref, 1 - core)):
            place = pl.ds(pl.multiple_of(side * half, half), half)
            target[0, :half] = dot(low_t[place, :], dpre[:, column]).astype(jnp.bfloat16)
            target[0, half:] = dot(dout_t[place, :], hidden_all[:, column]).astype(jnp.bfloat16)


def input_grad_kernel(spacing, places, scalars, dconv_ref, dmid_ref, *refs):
    count = 2 * len(places)
    grad_ref, weight, padded, sem = refs[count:]
    rows = dconv_ref.shape[0]
    margin = (padded.shape[0] - rows) // 2
    copies = conv_copies(scalars, places, refs[:count], weight, sem)
    spread(padded, dconv_ref[...].astype(jnp.float32), spacing)
    for copy in copies:
        copy.wait()
    total = jnp.zeros((rows, D), jnp.float32)
    for tap in range(TAPS):
        shifted = padded[pl.ds(margin - (tap - 4) * spacing, rows), :].astype(jnp.bfloat16)
        total = total + dot(shifted, weight[pl.ds(tap * D, D), :], ((1,), (1,)))
    mask = row_mask(0, rows, scalars[0])
    grad_ref[...] = (dmid_ref[...] + mask * total).astype(jnp.bfloat16)


def conv_terms(scalars, spacing, refs, targets, scratch):
    x_ref, dconv_ref = refs
    padded, xt, kept, sent, sem = scratch
    own, core = scalars[1], scalars[2]
    rows = x_ref.shape[0]
    margin = (padded.shape[0] - rows) // 2
    chunk, wide = targets[0].shape[1:]
    block = math.gcd(chunk, D)
    masked = x_ref[...].astype(jnp.float32) * row_mask(0, rows, scalars[0])
    xt[...] = masked.astype(jnp.bfloat16).T
    spread(padded, dconv_ref[...].astype(jnp.float32), spacing)
    leaving = []
    for tap in range(TAPS):
        shifted = padded[pl.ds(margin - (tap - 4) * spacing, rows), :].astype(jnp.bfloat16)
        grad = dot(xt[...], shifted)
        left, right = grad[:, :wide].astype(jnp.bfloat16), grad[:, wide:].astype(jnp.bfloat16)
        kept[tap] = jnp.where(core == 0, left, right)
        sent[tap] = jnp.where(core == 0, right, left)
        for part in range(D // block):
            row = tap * D + part * block
            place = own ^ (row // chunk)
            for source, target in zip((kept, sent), targets):
                copy = pltpu.make_async_copy(
                    source.at[tap, pl.ds(part * block, block), :],
                    target.at[place, pl.ds(row % chunk, block), :],
                    sem,
                )
                copy.start()
                leaving.append(copy)
    return leaving


def conv_terms_kernel(spacing, scalars, x_ref, dconv_ref, keep_hbm, send_hbm, *scratch):
    for copy in conv_terms(scalars, spacing, (x_ref, dconv_ref), (keep_hbm, send_hbm), scratch):
        copy.wait()


def conv_grad_kernel(spacing, places, scalars, x_ref, dconv_ref, dmid_hbm, *refs):
    count = 2 * len(places)
    keep_hbm, send_hbm, grad_ref = refs[count : count + 3]
    weight, padded, xt, kept, sent, dmid, sems = refs[count + 3 :]
    rows = x_ref.shape[0]
    margin = (padded.shape[0] - rows) // 2
    weights = conv_copies(scalars, places, refs[:count], weight, sems.at[0])
    residual = pltpu.make_async_copy(dmid_hbm, dmid, sems.at[1])
    residual.start()
    leaving = conv_terms(
        scalars,
        spacing,
        (x_ref, dconv_ref),
        (keep_hbm, send_hbm),
        (padded, xt, kept, sent, sems.at[2]),
    )
    for copy in weights:
        copy.wait()
    total = jnp.zeros((rows, D), jnp.float32)
    for tap in range(TAPS):
        shifted = padded[pl.ds(margin - (tap - 4) * spacing, rows), :].astype(jnp.bfloat16)
        total = total + dot(shifted, weight[pl.ds(tap * D, D), :], ((1,), (1,)))
    residual.wait()
    mask = row_mask(0, rows, scalars[0])
    grad_ref[...] = (dmid[...] + mask * total).astype(jnp.bfloat16)
    for copy in leaving:
        copy.wait()


def split_low(value):
    high = value.astype(jnp.bfloat16)
    return high, (value - high.astype(jnp.float32)).astype(jnp.bfloat16)


def mul_same(left, right):
    half = left[0].shape[0] // 2

    def part(rows, columns):
        (a, b), (c, d) = [m[rows] for m in left], [m[:, columns] for m in right]
        return dot(a, c) + (dot(a, d) + dot(b, c))

    upper = part(slice(0, half), slice(None))
    corner = part(slice(half, None), slice(half, None))
    lower = jnp.concatenate([upper[:, half:].T, corner], axis=1)
    return jnp.concatenate([upper, lower], axis=0)


def tiles_of(rows):
    count = rows // LANES
    return [(i, j) for i in range(count) for j in range(i, count)]


def pack(gram, first_ref, second_ref):
    places = tiles_of(gram.shape[0])
    half = len(places) // 2
    for index, (i, j) in enumerate(places):
        tile_values = gram[i * LANES : (i + 1) * LANES, j * LANES : (j + 1) * LANES]
        ref, place = (first_ref, index) if index < half else (second_ref, index - half)
        ref[place] = tile_values


def unpack(first_refs, second_refs, rows):
    count = rows // LANES
    found = {}
    half = first_refs[0].shape[0]
    for index, (i, j) in enumerate(tiles_of(rows)):
        refs, place = (first_refs, index) if index < half else (second_refs, index - half)
        values = refs[0][place]
        for ref in refs[1:]:
            values = values + ref[place]
        found[i, j] = values
        if i != j:
            found[j, i] = values.T
    return jnp.concatenate(
        [jnp.concatenate([found[i, j] for j in range(count)], axis=1) for i in range(count)], axis=0
    )


def schulz_kernel(first_refs, second_refs, turn_ref):
    rows = turn_ref.shape[0]
    eye = (
        lax.broadcasted_iota(jnp.int32, (rows, rows), 0)
        == lax.broadcasted_iota(jnp.int32, (rows, rows), 1)
    ).astype(jnp.float32)
    raw = unpack(first_refs, second_refs, rows)
    trace = jnp.sum(jnp.sum(raw * eye, axis=0, keepdims=True), axis=1, keepdims=True)
    scale = lax.rsqrt(trace + GRAM_EPSILON)
    gram, turn = raw * (scale * scale), None
    for sweep in range(5):
        parts = split_low(gram)
        square = mul_same(parts, parts)
        poly = split_low(SCHULZ_LINEAR * eye + SCHULZ_CUBIC * gram + SCHULZ_QUINTIC * square)
        if sweep == 0:
            turn = poly
        elif sweep < 4:
            turn = split_low(mul_same(turn, poly))
        else:
            turn_ref[...] = mul_same(turn, poly) * scale
        if sweep < 4:
            gram = mul_same(parts, split_low(mul_same(poly, poly)))


def split_sums_kernel(bits, *refs):
    for part in range(2):
        (one, first_one), (two, first_two) = [
            (ref, first) for ref, first in zip(refs[2 * part : 2 * part + 2], bits[part][1])
        ]
        sent, kept = refs[4 + 2 * part : 6 + 2 * part]
        bit, rows = bits[part][0], sent.shape[1]
        counts = {False: 0, True: 0}
        for place, key in enumerate(bits[part][2]):
            leaves = bool(key & bit)
            value = one[place, pl.ds(first_one, rows), :].astype(jnp.float32) + two[
                place, pl.ds(first_two, rows), :
            ].astype(jnp.float32)
            (sent if leaves else kept)[counts[leaves]] = value.astype(jnp.bfloat16)
            counts[leaves] += 1


def last_sums_kernel(steps, scalars, *refs):
    *terms, total = refs[:4] + refs[-1:]
    targets = refs[4:-1]
    rows = terms[0].shape[1]
    for part in range(2):
        one, two = terms[2 * part : 2 * part + 2]
        total[pl.ds(part * rows, rows), :] = one[0].astype(jnp.float32) + two[0].astype(jnp.float32)
    share = targets[0].shape[0]
    for step, target in enumerate(targets):
        place = lax.rem(scalars[0] + step, steps)
        target[...] = total[pl.ds(pl.multiple_of(place * share, 8), share), :].astype(jnp.bfloat16)


def add_all_kernel(*refs):
    total = refs[0][...].astype(jnp.float32)
    for ref in refs[1:-1]:
        total = total + ref[...].astype(jnp.float32)
    refs[-1][...] = total.astype(jnp.bfloat16)


def add_cores_kernel(scalars, keep_ref, got_ref, out_ref):
    value = keep_ref[...].astype(jnp.float32) + got_ref[...].astype(jnp.float32)
    out_ref[...] = value.astype(jnp.bfloat16)


def join_parts_kernel(count, scalars, *refs):
    mine, other = refs[-2:]
    share = refs[0].shape[0]
    me, core = scalars[0], scalars[1]
    for step in range(count):
        place = pl.ds(pl.multiple_of(lax.rem(me + count - step, count) * share, 16), share)
        first, second = refs[step][...], refs[count][place, :]
        mine[place, :] = jnp.where(core == 0, first, second)
        other[place, :] = jnp.where(core == 0, second, first)


def conv_state_kernel(
    scalars, mine_ref, got_ref, moment_ref, grad_ref, state_ref, first_ref, second_ref, high, cross
):
    step = pl.program_id(0)
    mine, got = mine_ref[...].astype(jnp.float32), got_ref[...].astype(jnp.float32)
    core = scalars[0]
    grad = jnp.concatenate(
        [jnp.where(core == 0, mine, got), jnp.where(core == 0, got, mine)], axis=1
    )
    grad_ref[...] = grad
    state = MUON_MOMENTUM * moment_ref[...] + grad
    state_ref[...] = state
    top, low = split_low(state)

    @pl.when(step == 0)
    def _():
        high[...] = jnp.zeros_like(high)
        cross[...] = jnp.zeros_like(cross)

    high[...] += dot(top, top, ((0,), (0,)))
    cross[...] += dot(top, low, ((0,), (0,)))

    @pl.when(step == pl.num_programs(0) - 1)
    def _():
        mixed = cross[...]
        pack(high[...] + (mixed + mixed.T), first_ref, second_ref)


def pair_state_kernel(
    scalars,
    mine_ref,
    got_ref,
    up_moment_ref,
    down_moment_ref,
    up_grad_ref,
    down_grad_ref,
    up_state_ref,
    down_state_ref,
    *packed,
):
    core = scalars[0]
    mine, got = mine_ref[...].astype(jnp.float32), got_ref[...].astype(jnp.float32)
    left, right = jnp.where(core == 0, mine, got), jnp.where(core == 0, got, mine)
    half = mine.shape[0] // 2
    grads = [
        jnp.concatenate([left[place], right[place]], axis=0)
        for place in (slice(0, half), slice(half, None))
    ]
    up_grad_ref[...] = grads[0]
    down_grad = grads[1].T
    down_grad_ref[...] = down_grad
    up_state = MUON_MOMENTUM * up_moment_ref[...] + grads[0]
    up_state_ref[...] = up_state
    down_state = MUON_MOMENTUM * down_moment_ref[...] + down_grad
    down_state_ref[...] = down_state
    for state, contract, refs in (
        (up_state, ((1,), (1,)), packed[:2]),
        (down_state, ((0,), (0,)), packed[2:]),
    ):
        top, low = split_low(state)
        mixed = dot(top, low, contract)
        pack(dot(top, top, contract) + (mixed + mixed.T), *refs)


def params(limit=VMEM_BYTES):
    return pltpu.CompilerParams(vmem_limit_bytes=limit)


def cost(macs, moved=8 << 20):
    return pl.CostEstimate(flops=2 * macs, bytes_accessed=moved, transcendentals=0)


ANY = pl.BlockSpec(memory_space=pl.ANY)


def whole(shape):
    return pl.BlockSpec(shape, lambda *_: (0,) * len(shape))


def tile(rows, wide):
    return pl.BlockSpec((rows, wide), lambda step, *_: (step, 0))


def shape_of(shape, dtype):
    return jax.ShapeDtypeStruct(shape, dtype)


def call(kernel, grid, in_specs, out_specs, out_shape, scratch, macs, after=(), limit=VMEM_BYTES):
    taken = 1 + len(in_specs)

    def body(*refs):
        kernel(*refs[:taken], *refs[taken + len(after) :])

    made = pl.pallas_call(
        body,
        grid_spec=pltpu.PrefetchScalarGridSpec(
            num_scalar_prefetch=1,
            grid=grid,
            in_specs=list(in_specs) + [ANY] * len(after),
            out_specs=out_specs,
            scratch_shapes=scratch,
        ),
        out_shape=out_shape,
        compiler_params=params(limit),
        cost_estimate=cost(macs),
    )
    return lambda *arrays: made(*arrays, *after)


def padded_scratch(win_len, spacing):
    margin = max(4 * spacing, 8)
    return pltpu.VMEM(
        (win_len + 2 * margin, D), jnp.bfloat16 if spacing % 16 == 0 else jnp.float32
    )


def conv_forward(scalars, x, vectors, gathered, block, after=()):
    spacing = SPACINGS[block]
    win_len = x.shape[0]
    rows = min(512, win_len)
    arrays, others, places = gathered
    arrays = arrays + others
    return call(
        functools.partial(conv_forward_kernel, spacing, places),
        (win_len // rows,),
        [whole(x.shape), whole(vectors.shape)] + [ANY] * len(arrays),
        [tile(rows, D)] * 4,
        [
            shape_of((win_len, D), jnp.bfloat16),
            shape_of((win_len, D), jnp.bfloat16),
            shape_of((win_len, D), jnp.float32),
            shape_of((win_len, D), jnp.bfloat16),
        ],
        [
            pltpu.VMEM((TAPS * D, D), jnp.bfloat16),
            padded_scratch(win_len, spacing),
            pltpu.SemaphoreType.DMA,
        ],
        win_len * TAPS * D * D,
        after,
        LESS_BYTES,
    )(scalars, x, vectors, *arrays)


def pair_scratch(groups, wide):
    return [pltpu.VMEM((groups, 2, D, wide), jnp.bfloat16), pltpu.SemaphoreType.DMA]


def pair_forward(scalars, middle, vectors, bias, head, head_bias, pair, block, after=()):
    win_len = middle.shape[0]
    rows = min(512, win_len)
    groups, wide = bias.shape
    return call(
        functools.partial(pair_forward_kernel, block),
        (win_len // rows,),
        [
            tile(rows, D),
            whole(vectors.shape),
            whole(bias.shape),
            whole(head.shape),
            whole(head_bias.shape),
        ]
        + [ANY] * 2,
        [tile(rows, D), tile(rows, LANES), tile(rows, D), whole((8, LANES))],
        [
            shape_of((win_len, D), jnp.bfloat16),
            shape_of((win_len, LANES), jnp.float32),
            shape_of((win_len, D), jnp.bfloat16),
            shape_of((8, LANES), jnp.float32),
        ],
        pair_scratch(groups, wide),
        win_len * 2 * D * FF,
        after,
        LESS_BYTES,
    )(scalars, middle, vectors, bias, head, head_bias, *pair)


def inner_backward(scalars, grad, norms, vectors, bias, saved, pair, block, forward, after=()):
    win_len = grad.shape[0]
    rows = min(512 if forward else 256, win_len)
    tiles = win_len // rows
    groups, wide = bias.shape

    def early(columns):
        return pl.BlockSpec((rows, columns), lambda step, *_: (jnp.minimum(step, tiles - 1), 0))

    place = pl.BlockSpec(
        (1, D, wide), lambda step, s: (jnp.maximum(step - tiles, 0) ^ s[1], 0, 0)
    )
    if forward:
        saved_specs = [early(D), whole(saved[1].shape), whole(saved[2].shape)]
    else:
        saved_specs = [early(D), early(D), early(LANES)]
    out_specs = [early(D), early(D), whole((16, D)), whole((groups, wide)), place, place]
    out_shapes = [
        shape_of((win_len, D), jnp.float32),
        shape_of((win_len, D), jnp.bfloat16),
        shape_of((16, D), jnp.float32),
        shape_of((groups, wide), jnp.float32),
        shape_of((groups, D, wide), jnp.bfloat16),
        shape_of((groups, D, wide), jnp.bfloat16),
    ]
    if forward:
        out_specs += [early(D), whole((8, LANES))]
        out_shapes += [shape_of((win_len, D), jnp.bfloat16), shape_of((8, LANES), jnp.float32)]
    weights, sem = pair_scratch(groups, wide)
    return call(
        functools.partial(inner_backward_kernel, block, tiles, forward),
        (tiles + groups,),
        [early(D), early(D), early(D), whole(vectors.shape), whole(bias.shape)]
        + saved_specs
        + [ANY] * 2,
        out_specs,
        out_shapes,
        [
            weights,
            pltpu.VMEM((rows, FF), jnp.bfloat16),
            pltpu.VMEM((win_len, FF), jnp.bfloat16),
            pltpu.VMEM((win_len, FF), jnp.bfloat16),
            pltpu.VMEM((D, win_len), jnp.bfloat16),
            pltpu.VMEM((D, win_len), jnp.bfloat16),
            sem,
        ],
        win_len * 4 * D * FF,
        after,
    )(scalars, grad, *norms, vectors, bias, *saved, *pair)


def conv_grad(scalars, x, d_conv, d_middle, gathered, block, groups, after=()):
    win_len = x.shape[0]
    chunk = TAPS * D // groups
    spacing = SPACINGS[block]
    arrays, others, places = gathered
    arrays = arrays + others
    return call(
        functools.partial(conv_grad_kernel, spacing, places),
        (1,),
        [whole(x.shape), whole(x.shape), ANY] + [ANY] * len(arrays),
        [ANY, ANY, whole(x.shape)],
        [shape_of((groups, chunk, D // 2), jnp.bfloat16)] * 2
        + [shape_of((win_len, D), jnp.bfloat16)],
        [
            pltpu.VMEM((TAPS * D, D), jnp.bfloat16),
            padded_scratch(win_len, spacing),
            pltpu.VMEM((D, win_len), jnp.bfloat16),
            pltpu.VMEM((TAPS, D, D // 2), jnp.bfloat16),
            pltpu.VMEM((TAPS, D, D // 2), jnp.bfloat16),
            pltpu.VMEM((win_len, D), jnp.float32),
            pltpu.SemaphoreType.DMA((3,)),
        ],
        win_len * 2 * TAPS * D * D,
        after,
    )(scalars, x, d_conv, d_middle, *arrays)


def conv_gradient(scalars, x, d_conv, block, groups, after=()):
    win_len = x.shape[0]
    chunk = TAPS * D // groups
    return call(
        functools.partial(conv_terms_kernel, SPACINGS[block]),
        (1,),
        [whole(x.shape), whole(x.shape)],
        [ANY, ANY],
        [shape_of((groups, chunk, D // 2), jnp.bfloat16)] * 2,
        [
            padded_scratch(win_len, SPACINGS[block]),
            pltpu.VMEM((D, win_len), jnp.bfloat16),
            pltpu.VMEM((TAPS, D, D // 2), jnp.bfloat16),
            pltpu.VMEM((TAPS, D, D // 2), jnp.bfloat16),
            pltpu.SemaphoreType.DMA,
        ],
        win_len * TAPS * D * D,
        after,
    )(scalars, x, d_conv)


def input_gradient(scalars, d_conv, d_middle, gathered, block, after=()):
    win_len = d_conv.shape[0]
    arrays, others, places = gathered
    arrays = arrays + others
    return call(
        functools.partial(input_grad_kernel, SPACINGS[block], places),
        (1,),
        [whole(d_conv.shape), whole(d_conv.shape)] + [ANY] * len(arrays),
        whole(d_conv.shape),
        shape_of((win_len, D), jnp.bfloat16),
        [
            pltpu.VMEM((TAPS * D, D), jnp.bfloat16),
            padded_scratch(win_len, SPACINGS[block]),
            pltpu.SemaphoreType.DMA,
        ],
        win_len * TAPS * D * D,
        after,
    )(scalars, d_conv, d_middle, *arrays)


def schulz(parts, after=()):
    first, second = parts

    def body(*refs):
        schulz_kernel(refs[: len(first)], refs[len(first) : len(first) + len(second)], refs[-1])

    arrays = [*first, *second]
    return pl.pallas_call(
        body,
        in_specs=[whole(array.shape) for array in arrays] + [ANY] * len(after),
        out_specs=whole((D, D)),
        out_shape=shape_of((D, D), jnp.float32),
        compiler_params=params(LESS_BYTES),
        cost_estimate=cost(17 * 3 * D * D * D),
    )(*arrays, *after)


def plain(kernel, arrays, out_shapes, scratch=(), scalars=None):
    if scalars is not None:
        return call(
            kernel,
            (1,),
            [whole(array.shape) for array in arrays],
            [whole(shape) for shape in out_shapes],
            [shape_of(shape, jnp.bfloat16) for shape in out_shapes],
            list(scratch),
            1 << 20,
            limit=LESS_BYTES,
        )(scalars, *arrays)
    return pl.pallas_call(
        kernel,
        out_shape=[shape_of(shape, jnp.bfloat16) for shape in out_shapes],
        compiler_params=params(LESS_BYTES),
        cost_estimate=cost(1 << 20),
    )(*arrays)


def split_sums(terms, rows, bits, keys):
    arrays = [array for part in terms for array, _ in part]
    plan = [
        (bit, [first for _, first in part], part_keys)
        for bit, part, part_keys in zip(bits, terms, keys)
    ]
    count, wide = arrays[0].shape[0], arrays[0].shape[2]
    outs = plain(
        functools.partial(split_sums_kernel, plan), arrays, [(count // 2, rows, wide)] * 4
    )
    return outs[0::2], outs[1::2]


def add_cores(own, keep, got):
    groups, rows, wide = keep.shape
    relative = pl.BlockSpec((1, rows, wide), lambda step, s: (step, 0, 0))
    return call(
        add_cores_kernel,
        (groups,),
        [relative, relative],
        pl.BlockSpec((1, rows, wide), lambda step, s: (step ^ s[0], 0, 0)),
        shape_of(keep.shape, jnp.bfloat16),
        [],
        1 << 20,
        limit=LESS_BYTES,
    )(own.reshape(1).astype(jnp.int32), keep, got)


def last_sums(me, terms, rows, count):
    arrays = [array for part in terms for array, _ in part]
    wide = arrays[0].shape[2]
    return plain(
        functools.partial(last_sums_kernel, count),
        arrays,
        [(2 * rows // count, wide)] * count,
        [pltpu.VMEM((2 * rows, wide), jnp.float32)],
        me.reshape(1).astype(jnp.int32),
    )


def add_all(arrays):
    return plain(add_all_kernel, arrays, [arrays[0].shape])[0]


def join_parts(scalars, first, second):
    count = len(first)
    share, wide = first[0].shape
    return plain(
        functools.partial(join_parts_kernel, count),
        [*first, second],
        [(count * share, wide)] * 2,
        (),
        scalars,
    )


def packed_shapes():
    count = len(tiles_of(D)) // 2
    return [(count, LANES, LANES)] * 2


def conv_states(core, mine, got, moment, after=()):
    chunk = moment.shape[0]
    rows = chunk // 3
    shapes = packed_shapes()
    return call(
        conv_state_kernel,
        (3,),
        [tile(rows, D // 2), tile(rows, D // 2), tile(rows, D)],
        [tile(rows, D), tile(rows, D)] + [whole(shape) for shape in shapes],
        [shape_of((chunk, D), jnp.float32)] * 2
        + [shape_of(shape, jnp.float32) for shape in shapes],
        [pltpu.VMEM((D, D), jnp.float32)] * 2,
        2 * chunk * D * D,
        after,
        LESS_BYTES,
    )(core, mine, got, moment)


def pair_states(core, mine, got, up_moment, down_moment, after=()):
    shapes = packed_shapes() * 2
    outs = [up_moment.shape, down_moment.shape] * 2 + shapes
    return call(
        pair_state_kernel,
        (1,),
        [whole(value.shape) for value in (mine, got, up_moment, down_moment)],
        [whole(shape) for shape in outs],
        [shape_of(shape, jnp.float32) for shape in outs],
        [],
        4 * up_moment.shape[1] * D * D,
        after,
        LESS_BYTES,
    )(core, mine, got, up_moment, down_moment)


def on_device(
    inputs,
    cotangent,
    lengths,
    species,
    conv_weight,
    up_weight,
    down_weight,
    conv_moment,
    up_moment,
    down_moment,
    vec_values,
    vec_first,
    vec_second,
    head_weight,
    head_bias,
):
    core = lax.axis_index("section")
    own = lax.axis_index("ns")
    groups = lax.axis_size("ns")
    feature = inputs.shape[2]
    wide = FF // groups

    half = feature // 2

    def conv_half(side):
        return lax.dynamic_slice_in_dim(conv_weight[0], side * half, half, 1).astype(jnp.bfloat16)

    pair_low = jnp.stack(
        [up_weight[0].astype(jnp.bfloat16), down_weight[0].astype(jnp.bfloat16).T]
    )

    def pair_half(side):
        return lax.dynamic_slice_in_dim(pair_low, side * half, half, 1)

    leaving = together([conv_half(1 - core), pair_half(1 - core)])
    conv_got, pair_got = together([swap_cores(value) for value in leaving])
    conv_mine, pair_mine = conv_half(core), pair_half(core)
    conv_parts = [
        jnp.where(core == block, conv_mine, conv_got) for block in range(2)
    ]
    pair_parts = [
        jnp.where(core == block, pair_mine, pair_got) for block in range(2)
    ]
    conv_tasks = [Task(gather_rows(part, "ns")) for part in conv_parts]
    pairs = lax.all_gather(jnp.stack(pair_parts), "ns")
    vectors = in_order(core, vec_values[0], swap_cores(vec_values[0]))
    finish(conv_tasks[0])
    pairs = together([pairs], conv_tasks[0].result[1][-1])[0]

    batches = inputs.shape[0] // 2
    win_len = inputs.shape[1]
    species_range = jnp.arange(SPECIES)
    classes = head_weight.shape[1]
    head = jnp.pad(head_weight, ((0, 0), (0, LANES - classes)))
    head_shift = jnp.pad(head_bias[None], ((0, 0), (0, LANES - classes)), constant_values=-1e30)
    prob_sums = [jnp.zeros((SPECIES, classes), jnp.float32)] * 2
    token_counts = jnp.zeros((SPECIES,), jnp.float32)
    kept = {}
    outputs = [[], []]
    input_grads = [[], []]

    def add_up(name, values):
        kept[name] = values if name not in kept else [a + b for a, b in zip(kept[name], values)]

    def own_windows(parts):
        mine = jnp.stack(parts[0]), jnp.stack(parts[1])
        (got,) = yield [(jnp.where(core == 0, mine[1], mine[0]), swap_cores)]
        joined = in_order(core, jnp.where(core == 0, mine[0], mine[1]), got)
        return joined.reshape((1, 2 * batches) + joined.shape[2:])

    for batch in range(batches):
        window = core * batches + batch
        length = at(lengths, window)
        scalars = jnp.stack([length, own, core]).astype(jnp.int32)
        species_hit = (species_range == at(species, window)).astype(jnp.float32)
        token_counts = token_counts + species_hit * length.astype(jnp.float32)
        values = at(inputs, window)
        last = batch == batches - 1
        norms, inputs_of = [], []
        for block in range(2):
            x = values
            if batch == 0 and block == 1:
                finish(conv_tasks[1])
            conv = [task.result for task in conv_tasks]

            def convolve(after=()):
                return conv_forward(scalars, x, vectors[block], conv[block], block, after=after)

            def feed_forward(after=()):
                return pair_forward(
                    scalars,
                    middle,
                    vectors[block],
                    bias,
                    head,
                    head_shift,
                    (pairs, others),
                    block,
                    after=after,
                )

            bias = vectors[block][3:7].reshape(groups, wide)
            early = batch == 0 and block == 0
            n1, slope1, middle, low = run([conv_tasks[1]], convolve) if early else convolve()
            if early:
                pairs = together([pairs], low)[0]
                others = together([swap_cores(pairs)])[0]
            norms.append((n1, slope1))
            inputs_of.append(x)
            if block == 1:
                break
            n2, scale2, values, probs = (
                run([conv_tasks[1]], feed_forward) if early else feed_forward()
            )
            outputs[0].append(values)
            prob_sums[0] = prob_sums[0] + species_hit[:, None] * probs[:1, :classes]
            saved = low, n2, scale2
        grad = at(cotangent, window)
        last = batch == batches - 1
        for block in (1, 0):
            x = inputs_of[block]
            bias = vectors[block][3:7].reshape(groups, wide)
            if block == 1:
                first_saved, saved = saved, (middle, head, head_shift)
            else:
                saved = first_saved

            def inner(after):
                return inner_backward(
                    scalars,
                    grad,
                    norms[block],
                    vectors[block],
                    bias,
                    saved,
                    (pairs, others),
                    block,
                    block == 1,
                    after=after,
                )

            def outer(after):
                return conv_grad(
                    scalars, x, d_conv, d_middle, conv[block], block, groups, after=after
                )

            if last and block == 0:
                conv_one = Task(sum_cores(own, *kept["conv", 1]))
                pair_one = lax.psum_scatter(pair_one.result, "ns", scatter_dimension=0)
                made = run([conv_one, shared_out], inner)
            else:
                made = inner(())
            if block == 1:
                *made, values, probs = made
                outputs[1].append(values)
                prob_sums[1] = prob_sums[1] + species_hit[:, None] * probs[:1, :classes]
            d_middle, d_conv, sums, bias_sums, *pair_terms = made
            add_up(("pair", block), pair_terms)
            vec_sums = jnp.concatenate(
                [sums[0:3], bias_sums.reshape(-1, feature), sums[7:10]]
            )
            add_up(("vec", block), [vec_sums])
            if last and block == 1:
                pair_one = Task(sum_cores(own, *kept["pair", 1]))
                shared_out = Task(own_windows(outputs))
                *terms, grad = run([pair_one], outer)
            elif last:
                pair_zero = Task(reduce_groups(*kept["pair", 0]))
                *terms, grad = run([pair_zero], outer, also=[pair_one])
            else:
                *terms, grad = outer(pair_terms)
            add_up(("conv", block), terms)
            input_grads[block].append(grad)

    conv_zero = Task(reduce_groups(*kept["conv", 0]))
    conv_one = together([conv_one.result], pair_one)[0]
    conv_one = lax.psum_scatter(conv_one, "ns", scatter_dimension=0)

    def small_parts(block):
        tail = jnp.concatenate([prob_sums[block].reshape(-1), token_counts])
        tail = jnp.pad(tail, (0, feature - tail.size))
        return jnp.concatenate([kept["vec", block][0], tail[None]])

    mine, theirs = small_parts(0), small_parts(1)
    small = Task(
        sum_small(jnp.where(core == 0, mine, theirs), jnp.where(core == 0, theirs, mine))
    )
    shared_in = Task(own_windows(input_grads))
    run([conv_zero, small])
    run([conv_zero, small], also=[conv_one])
    conv_one, pair_one = together([conv_one, pair_one], conv_zero.wanted[0][0])
    conv_one, pair_one = lax.psum((conv_one, pair_one), "dp")
    run([conv_zero, pair_zero, small])
    run([conv_zero, pair_zero, small])
    run([conv_zero, pair_zero, small])
    finish(conv_zero, pair_zero)
    place = jnp.stack([lax.axis_index("dp"), core]).astype(jnp.int32)
    core_scalar = place[1:]
    conv_one, pair_one = together([conv_one, pair_one], conv_zero.result[0])
    conv_all = Task(own_block(*join_parts(place, conv_zero.result, conv_one)))
    run([conv_all, pair_zero, small])
    pair_all = Task(own_block(*join_parts(place, finish(pair_zero), pair_one)))
    conv_total, conv_state, *conv_gram = run(
        [pair_all, small],
        lambda after: conv_states(core_scalar, *conv_all.result, conv_moment[0], after),
    )
    conv_gram = Task(sum_both_ways(conv_gram, "ns"))
    up_grad, down_grad, up_state, down_state, *grams = run(
        [conv_gram, small],
        lambda after: pair_states(
            core_scalar, *pair_all.result, up_moment[0], down_moment[0], after
        ),
    )
    up_gram = Task(sum_both_ways(grams[:2], "ns"))
    down_gram = Task(sum_both_ways(grams[2:], "ns"))
    run([conv_gram, up_gram, small])
    gram = finish(conv_gram)
    (conv_turn,) = run([up_gram, down_gram], lambda after: [schulz(gram, after)])
    gram = finish(up_gram)
    (up_turn,) = run([down_gram], lambda after: [schulz(gram, after)])
    gram = finish(down_gram)
    (down_turn,) = run([shared_in, small], lambda after: [schulz(gram, after)])
    activations, input_grad, small = shared_out.result, shared_in.result, finish(small)
    vec_grad = small[:-1]
    prob_total = small[-1, : prob_sums[0].size].reshape(prob_sums[0].shape)
    count_total = small[-1, prob_sums[0].size : prob_sums[0].size + SPECIES]

    def product(left, right, contract):
        return lax.dot_general(
            left,
            right,
            (contract, ((), ())),
            precision=lax.Precision.HIGH,
            preferred_element_type=jnp.float32,
        )

    up_orth = product(up_turn, up_state, ((0,), (0,)))
    down_orth = product(down_state, down_turn, ((1,), (0,)))
    conv_orth = product(conv_state, conv_turn, ((1,), (0,)))
    keep_factor = 1.0 - MUON_RATE * MUON_DECAY
    conv_next = conv_weight[0] * keep_factor - MUON_RATE * 0.2 * math.sqrt(9 * D) * conv_orth
    up_next = up_weight[0] * keep_factor - MUON_RATE * 0.2 * math.sqrt(FF) * up_orth
    down_next = down_weight[0] * keep_factor - MUON_RATE * 0.2 * math.sqrt(FF) * down_orth
    first_next = BETA_ONE * vec_first[0] + (1.0 - BETA_ONE) * vec_grad
    second_next = BETA_TWO * vec_second[0] + (1.0 - BETA_TWO) * vec_grad * vec_grad
    vec_next = vec_values[0] * (1.0 - ADAM_RATE * ADAM_DECAY) - ADAM_RATE * (
        first_next / (1.0 - BETA_ONE**STEP)
    ) / (jnp.sqrt(second_next / (1.0 - BETA_TWO**STEP)) + ADAM_EPSILON)
    species_freq = prob_total / jnp.maximum(count_total, 1.0)[:, None]
    species_share = SPECIES * count_total / jnp.sum(count_total)
    return (
        activations,
        input_grad,
        conv_total[None],
        up_grad[None],
        down_grad[None],
        conv_state[None],
        up_state[None],
        down_state[None],
        conv_next[None],
        up_next[None],
        down_next[None],
        conv_next.astype(jnp.bfloat16)[None],
        up_next.astype(jnp.bfloat16)[None],
        down_next.astype(jnp.bfloat16)[None],
        vec_grad[None],
        first_next[None],
        second_next[None],
        vec_next[None],
        species_freq[None],
        species_share[None],
    )


def solution(mesh):
    placed = (
        P(("dp", "ns"), None, None),
        P(("dp", "ns"), None, None),
        P(("dp", "ns")),
        P(("dp", "ns")),
        P("section", "ns", None),
        P("section", None, "ns"),
        P("section", "ns", None),
        P("section", "ns", None),
        P("section", None, "ns"),
        P("section", "ns", None),
        P("section", None, None),
        P("section", None, None),
        P("section", None, None),
        P(),
        P(),
    )
    return jax.shard_map(
        on_device,
        mesh=mesh,
        in_specs=placed,
        out_specs=(
            P("section", ("dp", "ns"), None, None),
            P("section", ("dp", "ns"), None, None),
            P("section", "ns", None),
            P("section", None, "ns"),
            P("section", "ns", None),
            P("section", "ns", None),
            P("section", None, "ns"),
            P("section", "ns", None),
            P("section", "ns", None),
            P("section", None, "ns"),
            P("section", "ns", None),
            P("section", "ns", None),
            P("section", None, "ns"),
            P("section", "ns", None),
            P("section", None, None),
            P("section", None, None),
            P("section", None, None),
            P("section", None, None),
            P("section", None, None),
            P("section", None),
        ),
        check_vma=False,
    )
```

```python
import functools
import math

import jax
import jax.numpy as jnp
from jax import lax
from jax.experimental import pallas as pl
from jax.experimental.pallas import tpu as pltpu
from jax.sharding import PartitionSpec as P

D = 512
FF = 2048
SECOND_DILATION = 32
SPECIES = 8
STEP = 10
TAPS = 9


NORM_EPSILON = 1e-05
GRAM_EPSILON = 1e-07
ADAM_EPSILON = 1e-08
SCHULZ_LINEAR = 3.4445
SCHULZ_CUBIC = -4.775
SCHULZ_QUINTIC = 2.0315
MUON_MOMENTUM = 0.5
MUON_RATE = 0.1
MUON_DECAY = 0.01
ADAM_RATE = 0.5
ADAM_DECAY = 0.01
BETA_ONE = 0.9
BETA_TWO = 0.95

SPACINGS = (1, SECOND_DILATION)
SWAP = [(0, 1), (1, 0)]
LANES = 128
VMEM_BYTES = 56 * 1024 * 1024
MORE_BYTES = 40 * 1024 * 1024
LESS_BYTES = 20 * 1024 * 1024
GELU_SCALE = 0.7978845608028654
GELU_CUBE = 0.044715


def swap_cores(value):
    return lax.ppermute(value, "section", SWAP)


def flip_bit(value, axis, bit):
    count = lax.axis_size(axis)
    return lax.ppermute(value, axis, [(source, source ^ bit) for source in range(count)])


def bits_of(axis):
    return [1 << power for power in range(int(math.log2(lax.axis_size(axis))))]


def turned(bits, part):
    start = part * len(bits) // 2
    return bits[start:] + bits[:start]


def at(array, index, axis=0):
    return lax.dynamic_index_in_dim(array, index, axis, keepdims=False)


def in_order(core, mine, other, axis=0):
    first = jnp.where(core == 0, mine, other)
    second = jnp.where(core == 0, other, mine)
    return jnp.stack([first, second], axis=axis)


def together(values, *fences):
    return lax.optimization_barrier((list(values), fences))[0]


class Task:
    def __init__(self, steps):
        self.steps = steps
        self.result = None
        self.wanted = next(steps)

    def give(self, got):
        try:
            self.wanted = self.steps.send(got)
        except StopIteration as end:
            self.wanted, self.result = None, end.value


def run(tasks, work=None, also=()):
    tasks = [task for task in tasks if task.wanted]
    wanted = [move for task in tasks for move in task.wanted]
    leaving = together([array for array, _ in wanted])
    made = work(leaving) if work else []
    arrived = [move(array) for array, (_, move) in zip(leaving, wanted)]
    arrived = together(arrived, made, also)
    for task in tasks:
        count = len(task.wanted)
        task.give(arrived[:count])
        arrived = arrived[count:]
    return made


def finish(task, *others):
    while task.wanted:
        run([task, *others])
    return task.result


def flips(axis, bit):
    return functools.partial(flip_bit, axis=axis, bit=bit)


def gather_rows(part, axis):
    half = part.shape[0] // 2
    held = [{0: rows} for rows in jnp.split(part, 2)]
    arrays, places, others = [part[None]], [[(0, 0)]], []
    fresh = arrays
    bits = [turned(bits_of(axis), part) for part in range(2)]
    for stage in range(len(bits[0]) + 1):
        moves = []
        last = stage == len(bits[0])
        if not last:
            for side in range(2):
                sent = jnp.stack([held[side][key] for key in sorted(held[side])])
                moves.append((sent, flips(axis, bits[side][stage])))
        moves += [(array, swap_cores) for array in fresh]
        got = yield moves
        others += got[len(got) - len(fresh) :]
        fresh = got[: len(got) - len(fresh)]
        arrays = arrays + fresh
        if not last:
            for side, array in enumerate(fresh):
                keys = sorted(held[side])
                bit = bits[side][stage]
                places.append([(key ^ bit, side * half) for key in keys])
                for place, key in enumerate(keys):
                    held[side][key ^ bit] = array[place]
    return arrays, others, places


def sum_cores(own, keep, send):
    (got,) = yield [(send, swap_cores)]
    return add_cores(own, keep, got)


def reduce_groups(keep, send):
    (got,) = yield [(send, swap_cores)]
    axis = "ns"
    bits = [turned(bits_of(axis), part) for part in range(2)]
    halves = keep.shape[1] // 2
    terms = [[(keep, part * halves), (got, part * halves)] for part in range(2)]
    keys = [list(range(keep.shape[0])) for part in range(2)]
    for stage in range(len(bits[0])):
        now = [bits[part][stage] for part in range(2)]
        sent, kept = split_sums(terms, halves, now, keys)
        keys = [[key for key in keys[part] if not key & now[part]] for part in range(2)]
        got = yield [(sent[part], flips(axis, bits[part][stage])) for part in range(2)]
        terms = [[(kept[part], 0), (got[part], 0)] for part in range(2)]
    axis = "dp"
    count = lax.axis_size(axis)
    me = lax.axis_index(axis)
    mine, *sent = last_sums(me, terms, halves, count)

    def move(step):
        moves = [(source, (source + step) % count) for source in range(count)]
        return lambda array: lax.ppermute(array, axis, moves)

    got = yield [(array, move(step + 1)) for step, array in enumerate(sent)]
    total = add_all([mine] + got)
    got = yield [(total, move(step)) for step in range(1, count)]
    return [total] + got


def sum_both_ways(parts, axis):
    for stage in range(len(bits_of(axis))):
        if stage:
            parts = [a + b for a, b in terms]
        got = yield [
            (value, flips(axis, turned(bits_of(axis), part)[stage]))
            for part, value in enumerate(parts)
        ]
        terms = list(zip(parts, got))
    return terms


def sum_small(value, other):
    (got,) = yield [(other, swap_cores)]
    value = value + got
    for axis in ("ns", "dp"):
        for bit in bits_of(axis):
            (got,) = yield [(value, flips(axis, bit))]
            value = value + got
    return value


def own_block(mine, other):
    (got,) = yield [(other, swap_cores)]
    return mine, got


def dot(left, right, contract=((1,), (0,))):
    return lax.dot_general(left, right, (contract, ((), ())), preferred_element_type=jnp.float32)


def gelu_parts(v):
    square = v * v
    bend = jnp.tanh(v * (GELU_SCALE + GELU_SCALE * GELU_CUBE * square))
    return 0.5 * v * (1.0 + bend), bend, square


def gelu_slope(v, bend, square):
    inner = GELU_SCALE + 3.0 * GELU_SCALE * GELU_CUBE * square
    return 0.5 * (1.0 + bend) + 0.5 * v * (1.0 - bend * bend) * inner


def normed(v):
    centred = v - jnp.mean(v, axis=-1, keepdims=True)
    scale = lax.rsqrt(jnp.mean(centred * centred, axis=-1, keepdims=True) + NORM_EPSILON)
    return centred * scale, scale


def norm_back(e, n, scale):
    return scale * (
        e - jnp.mean(e, axis=-1, keepdims=True) - n * jnp.mean(e * n, axis=-1, keepdims=True)
    )


def row_mask(first, rows, length):
    place = first + lax.broadcasted_iota(jnp.int32, (rows, 1), 0)
    return (place < length).astype(jnp.float32)


def start_all(copies):
    for copy in copies:
        copy.start()
    for copy in copies:
        copy.wait()


def conv_copies(scalars, places, refs, weight, sem):
    copies = []
    for side in range(2):
        for index, blocks in enumerate(places):
            ref = refs[side * len(places) + index]
            rows, wide = ref.shape[1:]
            column = (scalars[2] if side == 0 else 1 - scalars[2]) * wide
            for inner, (key, first) in enumerate(blocks):
                row = (scalars[1] ^ key) * refs[0].shape[1] + first
                target = weight.at[
                    pl.ds(pl.multiple_of(row, 16), rows),
                    pl.ds(pl.multiple_of(column, LANES), wide),
                ]
                copies.append(pltpu.make_async_copy(ref.at[inner], target, sem))
    for copy in copies:
        copy.start()
    return copies


def pair_copies(scalars, block, refs, weights, sem):
    copies = []
    for side, ref in enumerate(refs):
        rows = ref.shape[3]
        row = (scalars[2] if side == 0 else 1 - scalars[2]) * rows
        target = weights.at[:, :, pl.ds(pl.multiple_of(row, 16), rows), :]
        copies.append(pltpu.make_async_copy(ref.at[:, block], target, sem))
    for copy in copies:
        copy.start()
    return copies


def spread(scratch, values, spacing):
    margin = (scratch.shape[0] - values.shape[0]) // 2
    rows = values.shape[0]
    zeros = jnp.zeros((margin, values.shape[1]), scratch.dtype)
    scratch[pl.ds(0, margin), :] = zeros
    scratch[pl.ds(margin + rows, margin), :] = zeros
    scratch[pl.ds(margin, rows), :] = values.astype(scratch.dtype)


def conv_forward_kernel(spacing, places, scalars, x_ref, v_ref, *refs):
    count = 2 * len(places)
    n_ref, slope_ref, mid_ref, low_ref, weight, padded, sem = refs[count:]
    step = pl.program_id(0)
    rows = mid_ref.shape[0]
    margin = (padded.shape[0] - x_ref.shape[0]) // 2

    @pl.when(step == 0)
    def _():
        copies = conv_copies(scalars, places, refs[:count], weight, sem)
        spread(
            padded,
            x_ref[...].astype(jnp.float32) * row_mask(0, x_ref.shape[0], scalars[0]),
            spacing,
        )
        for copy in copies:
            copy.wait()

    first = pl.multiple_of(step * rows, rows)
    total = jnp.zeros(mid_ref.shape, jnp.float32)
    for tap in range(TAPS):
        shift = margin + (tap - 4) * spacing
        if spacing % 16 == 0:
            piece = padded[pl.ds(pl.multiple_of(first + shift, 16), rows), :]
        else:
            piece = pltpu.roll(padded[pl.ds(first, rows + 2 * margin), :], rows + 2 * margin - shift, 0)
            piece = piece[:rows].astype(jnp.bfloat16)
        total = total + dot(piece, weight[pl.ds(tap * D, D), :])
    total = total + v_ref[0:1, :]
    active, bend, square = gelu_parts(total)
    n, scale = normed(active)
    n_ref[...] = n.astype(jnp.bfloat16)
    slope_ref[...] = (gelu_slope(total, bend, square) * scale).astype(jnp.bfloat16)
    middle = (
        x_ref[pl.ds(first, rows), :].astype(jnp.float32) + n * v_ref[1:2, :] + v_ref[2:3, :]
    )
    mid_ref[...] = middle
    low_ref[...] = middle.astype(jnp.bfloat16)


def feed_forward_end(scalars, first, total, middle, v_ref, head_ref, head_bias_ref, prob_ref):
    n, scale = normed(total + v_ref[7:8, :])
    out = (middle + n * v_ref[8:9, :] + v_ref[9:10, :]).astype(jnp.bfloat16)
    logits = dot(out, head_ref[...]) + head_bias_ref[0:1, :]
    logits = logits - jnp.max(logits, axis=-1, keepdims=True)
    weights = jnp.exp(logits)
    chances = weights / jnp.sum(weights, axis=-1, keepdims=True)
    chances = chances * row_mask(first, middle.shape[0], scalars[0])
    prob_ref[...] += jnp.broadcast_to(jnp.sum(chances, axis=0, keepdims=True), prob_ref.shape)
    return n, scale, out


def pair_forward_kernel(
    block, scalars, mid_ref, v_ref, bias_ref, head_ref, head_bias_ref, own_ref, other_ref, *refs
):
    n_ref, scale_ref, out_ref, prob_ref, weights, sem = refs
    step = pl.program_id(0)
    rows = mid_ref.shape[0]

    @pl.when(step == 0)
    def _():
        copies = pair_copies(scalars, block, (own_ref, other_ref), weights, sem)
        prob_ref[...] = jnp.zeros_like(prob_ref)
        for copy in copies:
            copy.wait()

    middle = mid_ref[...]
    low = middle.astype(jnp.bfloat16)
    total = jnp.zeros(middle.shape, jnp.float32)
    for group in range(weights.shape[0]):
        pre = dot(low, weights[group, 0]) + bias_ref[group : group + 1, :]
        hidden = gelu_parts(pre)[0].astype(jnp.bfloat16)
        total = total + dot(hidden, weights[group, 1], ((1,), (1,)))
    n, scale, out = feed_forward_end(
        scalars, step * rows, total, middle, v_ref, head_ref, head_bias_ref, prob_ref
    )
    n_ref[...] = n.astype(jnp.bfloat16)
    scale_ref[...] = jnp.broadcast_to(scale, scale_ref.shape)
    out_ref[...] = out


def inner_backward_kernel(block, tiles, forward, scalars, *refs):
    grad_ref, n1_ref, slope1_ref, v_ref, bias_ref, *refs = refs
    if forward:
        mid_ref, head_ref, head_bias_ref, *refs = refs
    else:
        low_ref, n2_ref, scale2_ref, *refs = refs
    own_ref, other_ref, *refs = refs
    dmid_ref, dconv_ref, sums_ref, bias_sums_ref, keep_ref, send_ref, *refs = refs
    if forward:
        out_ref, prob_ref, *refs = refs
    weights, slopes, hidden_all, dpre, dout_t, low_t, sem = refs
    step = pl.program_id(0)
    rows = grad_ref.shape[0]
    groups, wide = weights.shape[0], weights.shape[3]

    def add_row(row, value):
        sums_ref[row : row + 1, :] += jnp.sum(value, axis=0, keepdims=True)

    @pl.when(step == 0)
    def _():
        copies = pair_copies(scalars, block, (own_ref, other_ref), weights, sem)
        sums_ref[...] = jnp.zeros_like(sums_ref)
        bias_sums_ref[...] = jnp.zeros_like(bias_sums_ref)
        if forward:
            prob_ref[...] = jnp.zeros_like(prob_ref)
        for copy in copies:
            copy.wait()

    @pl.when(step < tiles)
    def _():
        first = pl.multiple_of(step * rows, rows)
        place = pl.ds(first, rows)
        low = mid_ref[...].astype(jnp.bfloat16) if forward else low_ref[...]
        low_t[:, place] = low.T
        total = jnp.zeros((rows, D), jnp.float32)
        for group in range(groups):
            column = pl.ds(group * wide, wide)
            pre = dot(low, weights[group, 0]) + bias_ref[group : group + 1, :]
            hidden, bend, square = gelu_parts(pre)
            hidden = hidden.astype(jnp.bfloat16)
            hidden_all[place, column] = hidden
            slopes[:, column] = gelu_slope(pre, bend, square).astype(jnp.bfloat16)
            if forward:
                total = total + dot(hidden, weights[group, 1], ((1,), (1,)))
        if forward:
            n, scale, out = feed_forward_end(
                scalars, first, total, mid_ref[...], v_ref, head_ref, head_bias_ref, prob_ref
            )
            out_ref[...] = out
        else:
            n, scale = n2_ref[...].astype(jnp.float32), scale2_ref[:, 0:1]
        grad = grad_ref[...].astype(jnp.float32) * row_mask(first, rows, scalars[0])
        add_row(8, grad * n)
        add_row(9, grad)
        d_out = norm_back(grad * v_ref[8:9, :], n, scale).astype(jnp.bfloat16)
        dout_t[:, place] = d_out.T
        add_row(7, d_out.astype(jnp.float32))
        d_middle = grad
        for group in range(groups):
            column = pl.ds(group * wide, wide)
            d_hidden = dot(d_out, weights[group, 1])
            d_pre = d_hidden * slopes[:, column].astype(jnp.float32)
            bias_sums_ref[group : group + 1, :] += jnp.sum(d_pre, axis=0, keepdims=True)
            d_pre = d_pre.astype(jnp.bfloat16)
            dpre[place, column] = d_pre
            d_middle = d_middle + dot(d_pre, weights[group, 0], ((1,), (1,)))
        dmid_ref[...] = d_middle
        n = n1_ref[...].astype(jnp.float32)
        add_row(1, d_middle * n)
        add_row(2, d_middle)
        d_conv = norm_back(d_middle * v_ref[1:2, :], n, slope1_ref[...].astype(jnp.float32))
        dconv_ref[...] = d_conv.astype(jnp.bfloat16)
        add_row(0, d_conv)

    @pl.when(step >= tiles)
    def _():
        core = scalars[2]
        half = low_t.shape[0] // 2
        column = pl.ds(pl.multiple_of((step - tiles) * wide, wide), wide)
        for target, side in ((keep_ref, core), (send_ref, 1 - core)):
            place = pl.ds(pl.multiple_of(side * half, half), half)
            target[0, :half] = dot(low_t[place, :], dpre[:, column]).astype(jnp.bfloat16)
            target[0, half:] = dot(dout_t[place, :], hidden_all[:, column]).astype(jnp.bfloat16)


def input_grad_kernel(spacing, places, scalars, dconv_ref, dmid_ref, *refs):
    count = 2 * len(places)
    grad_ref, weight, padded, sem = refs[count:]
    rows = dconv_ref.shape[0]
    margin = (padded.shape[0] - rows) // 2
    copies = conv_copies(scalars, places, refs[:count], weight, sem)
    spread(padded, dconv_ref[...].astype(jnp.float32), spacing)
    for copy in copies:
        copy.wait()
    total = jnp.zeros((rows, D), jnp.float32)
    for tap in range(TAPS):
        shifted = padded[pl.ds(margin - (tap - 4) * spacing, rows), :].astype(jnp.bfloat16)
        total = total + dot(shifted, weight[pl.ds(tap * D, D), :], ((1,), (1,)))
    mask = row_mask(0, rows, scalars[0])
    grad_ref[...] = (dmid_ref[...] + mask * total).astype(jnp.bfloat16)


def conv_terms(scalars, spacing, refs, targets, scratch):
    x_ref, dconv_ref = refs
    padded, xt, kept, sent, sem = scratch
    own, core = scalars[1], scalars[2]
    rows = x_ref.shape[0]
    margin = (padded.shape[0] - rows) // 2
    chunk, wide = targets[0].shape[1:]
    block = math.gcd(chunk, D)
    masked = x_ref[...].astype(jnp.float32) * row_mask(0, rows, scalars[0])
    xt[...] = masked.astype(jnp.bfloat16).T
    spread(padded, dconv_ref[...].astype(jnp.float32), spacing)
    leaving = []
    for tap in range(TAPS):
        shifted = padded[pl.ds(margin - (tap - 4) * spacing, rows), :].astype(jnp.bfloat16)
        grad = dot(xt[...], shifted)
        left, right = grad[:, :wide].astype(jnp.bfloat16), grad[:, wide:].astype(jnp.bfloat16)
        kept[tap] = jnp.where(core == 0, left, right)
        sent[tap] = jnp.where(core == 0, right, left)
        for part in range(D // block):
            row = tap * D + part * block
            place = own ^ (row // chunk)
            for source, target in zip((kept, sent), targets):
                copy = pltpu.make_async_copy(
                    source.at[tap, pl.ds(part * block, block), :],
                    target.at[place, pl.ds(row % chunk, block), :],
                    sem,
                )
                copy.start()
                leaving.append(copy)
    return leaving


def conv_terms_kernel(spacing, scalars, x_ref, dconv_ref, keep_hbm, send_hbm, *scratch):
    for copy in conv_terms(scalars, spacing, (x_ref, dconv_ref), (keep_hbm, send_hbm), scratch):
        copy.wait()


def conv_grad_kernel(spacing, places, scalars, x_ref, dconv_ref, dmid_hbm, *refs):
    count = 2 * len(places)
    keep_hbm, send_hbm, grad_ref = refs[count : count + 3]
    weight, padded, xt, kept, sent, dmid, sems = refs[count + 3 :]
    rows = x_ref.shape[0]
    margin = (padded.shape[0] - rows) // 2
    weights = conv_copies(scalars, places, refs[:count], weight, sems.at[0])
    residual = pltpu.make_async_copy(dmid_hbm, dmid, sems.at[1])
    residual.start()
    leaving = conv_terms(
        scalars,
        spacing,
        (x_ref, dconv_ref),
        (keep_hbm, send_hbm),
        (padded, xt, kept, sent, sems.at[2]),
    )
    for copy in weights:
        copy.wait()
    total = jnp.zeros((rows, D), jnp.float32)
    for tap in range(TAPS):
        shifted = padded[pl.ds(margin - (tap - 4) * spacing, rows), :].astype(jnp.bfloat16)
        total = total + dot(shifted, weight[pl.ds(tap * D, D), :], ((1,), (1,)))
    residual.wait()
    mask = row_mask(0, rows, scalars[0])
    grad_ref[...] = (dmid[...] + mask * total).astype(jnp.bfloat16)
    for copy in leaving:
        copy.wait()


def split_low(value):
    high = value.astype(jnp.bfloat16)
    return high, (value - high.astype(jnp.float32)).astype(jnp.bfloat16)


def mul_same(left, right):
    half = left[0].shape[0] // 2

    def part(rows, columns):
        (a, b), (c, d) = [m[rows] for m in left], [m[:, columns] for m in right]
        return dot(a, c) + (dot(a, d) + dot(b, c))

    upper = part(slice(0, half), slice(None))
    corner = part(slice(half, None), slice(half, None))
    lower = jnp.concatenate([upper[:, half:].T, corner], axis=1)
    return jnp.concatenate([upper, lower], axis=0)


def tiles_of(rows):
    count = rows // LANES
    return [(i, j) for i in range(count) for j in range(i, count)]


def pack(gram, first_ref, second_ref):
    places = tiles_of(gram.shape[0])
    half = len(places) // 2
    for index, (i, j) in enumerate(places):
        tile_values = gram[i * LANES : (i + 1) * LANES, j * LANES : (j + 1) * LANES]
        ref, place = (first_ref, index) if index < half else (second_ref, index - half)
        ref[place] = tile_values


def unpack(first_refs, second_refs, rows):
    count = rows // LANES
    found = {}
    half = first_refs[0].shape[0]
    for index, (i, j) in enumerate(tiles_of(rows)):
        refs, place = (first_refs, index) if index < half else (second_refs, index - half)
        values = refs[0][place]
        for ref in refs[1:]:
            values = values + ref[place]
        found[i, j] = values
        if i != j:
            found[j, i] = values.T
    return jnp.concatenate(
        [jnp.concatenate([found[i, j] for j in range(count)], axis=1) for i in range(count)], axis=0
    )


def schulz_kernel(first_refs, second_refs, turn_ref):
    rows = turn_ref.shape[0]
    eye = (
        lax.broadcasted_iota(jnp.int32, (rows, rows), 0)
        == lax.broadcasted_iota(jnp.int32, (rows, rows), 1)
    ).astype(jnp.float32)
    raw = unpack(first_refs, second_refs, rows)
    trace = jnp.sum(jnp.sum(raw * eye, axis=0, keepdims=True), axis=1, keepdims=True)
    scale = lax.rsqrt(trace + GRAM_EPSILON)
    gram, turn = raw * (scale * scale), None
    for sweep in range(5):
        parts = split_low(gram)
        square = mul_same(parts, parts)
        poly = split_low(SCHULZ_LINEAR * eye + SCHULZ_CUBIC * gram + SCHULZ_QUINTIC * square)
        if sweep == 0:
            turn = poly
        elif sweep < 4:
            turn = split_low(mul_same(turn, poly))
        else:
            turn_ref[...] = mul_same(turn, poly) * scale
        if sweep < 4:
            gram = mul_same(parts, split_low(mul_same(poly, poly)))


def split_sums_kernel(bits, *refs):
    for part in range(2):
        (one, first_one), (two, first_two) = [
            (ref, first) for ref, first in zip(refs[2 * part : 2 * part + 2], bits[part][1])
        ]
        sent, kept = refs[4 + 2 * part : 6 + 2 * part]
        bit, rows = bits[part][0], sent.shape[1]
        counts = {False: 0, True: 0}
        for place, key in enumerate(bits[part][2]):
            leaves = bool(key & bit)
            value = one[place, pl.ds(first_one, rows), :].astype(jnp.float32) + two[
                place, pl.ds(first_two, rows), :
            ].astype(jnp.float32)
            (sent if leaves else kept)[counts[leaves]] = value.astype(jnp.bfloat16)
            counts[leaves] += 1


def last_sums_kernel(steps, scalars, *refs):
    *terms, total = refs[:4] + refs[-1:]
    targets = refs[4:-1]
    rows = terms[0].shape[1]
    for part in range(2):
        one, two = terms[2 * part : 2 * part + 2]
        total[pl.ds(part * rows, rows), :] = one[0].astype(jnp.float32) + two[0].astype(jnp.float32)
    share = targets[0].shape[0]
    for step, target in enumerate(targets):
        place = lax.rem(scalars[0] + step, steps)
        target[...] = total[pl.ds(pl.multiple_of(place * share, 8), share), :].astype(jnp.bfloat16)


def add_all_kernel(*refs):
    total = refs[0][...].astype(jnp.float32)
    for ref in refs[1:-1]:
        total = total + ref[...].astype(jnp.float32)
    refs[-1][...] = total.astype(jnp.bfloat16)


def add_cores_kernel(scalars, keep_ref, got_ref, out_ref):
    value = keep_ref[...].astype(jnp.float32) + got_ref[...].astype(jnp.float32)
    out_ref[...] = value.astype(jnp.bfloat16)


def join_parts_kernel(count, scalars, *refs):
    mine, other = refs[-2:]
    share = refs[0].shape[0]
    me, core = scalars[0], scalars[1]
    for step in range(count):
        place = pl.ds(pl.multiple_of(lax.rem(me + count - step, count) * share, 16), share)
        first, second = refs[step][...], refs[count][place, :]
        mine[place, :] = jnp.where(core == 0, first, second)
        other[place, :] = jnp.where(core == 0, second, first)


def conv_state_kernel(
    scalars, mine_ref, got_ref, moment_ref, grad_ref, state_ref, first_ref, second_ref, high, cross
):
    step = pl.program_id(0)
    mine, got = mine_ref[...].astype(jnp.float32), got_ref[...].astype(jnp.float32)
    core = scalars[0]
    grad = jnp.concatenate(
        [jnp.where(core == 0, mine, got), jnp.where(core == 0, got, mine)], axis=1
    )
    grad_ref[...] = grad
    state = MUON_MOMENTUM * moment_ref[...] + grad
    state_ref[...] = state
    top, low = split_low(state)

    @pl.when(step == 0)
    def _():
        high[...] = jnp.zeros_like(high)
        cross[...] = jnp.zeros_like(cross)

    high[...] += dot(top, top, ((0,), (0,)))
    cross[...] += dot(top, low, ((0,), (0,)))

    @pl.when(step == pl.num_programs(0) - 1)
    def _():
        mixed = cross[...]
        pack(high[...] + (mixed + mixed.T), first_ref, second_ref)


def pair_state_kernel(
    scalars,
    mine_ref,
    got_ref,
    up_moment_ref,
    down_moment_ref,
    up_grad_ref,
    down_grad_ref,
    up_state_ref,
    down_state_ref,
    *packed,
):
    core = scalars[0]
    mine, got = mine_ref[...].astype(jnp.float32), got_ref[...].astype(jnp.float32)
    left, right = jnp.where(core == 0, mine, got), jnp.where(core == 0, got, mine)
    half = mine.shape[0] // 2
    grads = [
        jnp.concatenate([left[place], right[place]], axis=0)
        for place in (slice(0, half), slice(half, None))
    ]
    up_grad_ref[...] = grads[0]
    down_grad = grads[1].T
    down_grad_ref[...] = down_grad
    up_state = MUON_MOMENTUM * up_moment_ref[...] + grads[0]
    up_state_ref[...] = up_state
    down_state = MUON_MOMENTUM * down_moment_ref[...] + down_grad
    down_state_ref[...] = down_state
    for state, contract, refs in (
        (up_state, ((1,), (1,)), packed[:2]),
        (down_state, ((0,), (0,)), packed[2:]),
    ):
        top, low = split_low(state)
        mixed = dot(top, low, contract)
        pack(dot(top, top, contract) + (mixed + mixed.T), *refs)


def params(limit=VMEM_BYTES):
    return pltpu.CompilerParams(vmem_limit_bytes=limit)


def cost(macs, moved=8 << 20):
    return pl.CostEstimate(flops=2 * macs, bytes_accessed=moved, transcendentals=0)


ANY = pl.BlockSpec(memory_space=pl.ANY)


def whole(shape):
    return pl.BlockSpec(shape, lambda *_: (0,) * len(shape))


def tile(rows, wide):
    return pl.BlockSpec((rows, wide), lambda step, *_: (step, 0))


def shape_of(shape, dtype):
    return jax.ShapeDtypeStruct(shape, dtype)


def call(kernel, grid, in_specs, out_specs, out_shape, scratch, macs, after=(), limit=VMEM_BYTES):
    taken = 1 + len(in_specs)

    def body(*refs):
        kernel(*refs[:taken], *refs[taken + len(after) :])

    made = pl.pallas_call(
        body,
        grid_spec=pltpu.PrefetchScalarGridSpec(
            num_scalar_prefetch=1,
            grid=grid,
            in_specs=list(in_specs) + [ANY] * len(after),
            out_specs=out_specs,
            scratch_shapes=scratch,
        ),
        out_shape=out_shape,
        compiler_params=params(limit),
        cost_estimate=cost(macs),
    )
    return lambda *arrays: made(*arrays, *after)


def padded_scratch(win_len, spacing):
    margin = max(4 * spacing, 8)
    return pltpu.VMEM(
        (win_len + 2 * margin, D), jnp.bfloat16 if spacing % 16 == 0 else jnp.float32
    )


def conv_forward(scalars, x, vectors, gathered, block, after=()):
    spacing = SPACINGS[block]
    win_len = x.shape[0]
    rows = min(512, win_len)
    arrays, others, places = gathered
    arrays = arrays + others
    return call(
        functools.partial(conv_forward_kernel, spacing, places),
        (win_len // rows,),
        [whole(x.shape), whole(vectors.shape)] + [ANY] * len(arrays),
        [tile(rows, D)] * 4,
        [
            shape_of((win_len, D), jnp.bfloat16),
            shape_of((win_len, D), jnp.bfloat16),
            shape_of((win_len, D), jnp.float32),
            shape_of((win_len, D), jnp.bfloat16),
        ],
        [
            pltpu.VMEM((TAPS * D, D), jnp.bfloat16),
            padded_scratch(win_len, spacing),
            pltpu.SemaphoreType.DMA,
        ],
        win_len * TAPS * D * D,
        after,
        LESS_BYTES,
    )(scalars, x, vectors, *arrays)


def pair_scratch(groups, wide):
    return [pltpu.VMEM((groups, 2, D, wide), jnp.bfloat16), pltpu.SemaphoreType.DMA]


def pair_forward(scalars, middle, vectors, bias, head, head_bias, pair, block, after=()):
    win_len = middle.shape[0]
    rows = min(512, win_len)
    groups, wide = bias.shape
    return call(
        functools.partial(pair_forward_kernel, block),
        (win_len // rows,),
        [
            tile(rows, D),
            whole(vectors.shape),
            whole(bias.shape),
            whole(head.shape),
            whole(head_bias.shape),
        ]
        + [ANY] * 2,
        [tile(rows, D), tile(rows, LANES), tile(rows, D), whole((8, LANES))],
        [
            shape_of((win_len, D), jnp.bfloat16),
            shape_of((win_len, LANES), jnp.float32),
            shape_of((win_len, D), jnp.bfloat16),
            shape_of((8, LANES), jnp.float32),
        ],
        pair_scratch(groups, wide),
        win_len * 2 * D * FF,
        after,
        LESS_BYTES,
    )(scalars, middle, vectors, bias, head, head_bias, *pair)


def inner_backward(scalars, grad, norms, vectors, bias, saved, pair, block, forward, after=()):
    win_len = grad.shape[0]
    rows = min(512 if forward else 256, win_len)
    tiles = win_len // rows
    groups, wide = bias.shape

    def early(columns):
        return pl.BlockSpec((rows, columns), lambda step, *_: (jnp.minimum(step, tiles - 1), 0))

    place = pl.BlockSpec(
        (1, D, wide), lambda step, s: (jnp.maximum(step - tiles, 0) ^ s[1], 0, 0)
    )
    if forward:
        saved_specs = [early(D), whole(saved[1].shape), whole(saved[2].shape)]
    else:
        saved_specs = [early(D), early(D), early(LANES)]
    out_specs = [early(D), early(D), whole((16, D)), whole((groups, wide)), place, place]
    out_shapes = [
        shape_of((win_len, D), jnp.float32),
        shape_of((win_len, D), jnp.bfloat16),
        shape_of((16, D), jnp.float32),
        shape_of((groups, wide), jnp.float32),
        shape_of((groups, D, wide), jnp.bfloat16),
        shape_of((groups, D, wide), jnp.bfloat16),
    ]
    if forward:
        out_specs += [early(D), whole((8, LANES))]
        out_shapes += [shape_of((win_len, D), jnp.bfloat16), shape_of((8, LANES), jnp.float32)]
    weights, sem = pair_scratch(groups, wide)
    return call(
        functools.partial(inner_backward_kernel, block, tiles, forward),
        (tiles + groups,),
        [early(D), early(D), early(D), whole(vectors.shape), whole(bias.shape)]
        + saved_specs
        + [ANY] * 2,
        out_specs,
        out_shapes,
        [
            weights,
            pltpu.VMEM((rows, FF), jnp.bfloat16),
            pltpu.VMEM((win_len, FF), jnp.bfloat16),
            pltpu.VMEM((win_len, FF), jnp.bfloat16),
            pltpu.VMEM((D, win_len), jnp.bfloat16),
            pltpu.VMEM((D, win_len), jnp.bfloat16),
            sem,
        ],
        win_len * 4 * D * FF,
        after,
        MORE_BYTES if forward else VMEM_BYTES,
    )(scalars, grad, *norms, vectors, bias, *saved, *pair)


def conv_grad(scalars, x, d_conv, d_middle, gathered, block, groups, after=()):
    win_len = x.shape[0]
    chunk = TAPS * D // groups
    spacing = SPACINGS[block]
    arrays, others, places = gathered
    arrays = arrays + others
    return call(
        functools.partial(conv_grad_kernel, spacing, places),
        (1,),
        [whole(x.shape), whole(x.shape), ANY] + [ANY] * len(arrays),
        [ANY, ANY, whole(x.shape)],
        [shape_of((groups, chunk, D // 2), jnp.bfloat16)] * 2
        + [shape_of((win_len, D), jnp.bfloat16)],
        [
            pltpu.VMEM((TAPS * D, D), jnp.bfloat16),
            padded_scratch(win_len, spacing),
            pltpu.VMEM((D, win_len), jnp.bfloat16),
            pltpu.VMEM((TAPS, D, D // 2), jnp.bfloat16),
            pltpu.VMEM((TAPS, D, D // 2), jnp.bfloat16),
            pltpu.VMEM((win_len, D), jnp.float32),
            pltpu.SemaphoreType.DMA((3,)),
        ],
        win_len * 2 * TAPS * D * D,
        after,
    )(scalars, x, d_conv, d_middle, *arrays)


def conv_gradient(scalars, x, d_conv, block, groups, after=()):
    win_len = x.shape[0]
    chunk = TAPS * D // groups
    return call(
        functools.partial(conv_terms_kernel, SPACINGS[block]),
        (1,),
        [whole(x.shape), whole(x.shape)],
        [ANY, ANY],
        [shape_of((groups, chunk, D // 2), jnp.bfloat16)] * 2,
        [
            padded_scratch(win_len, SPACINGS[block]),
            pltpu.VMEM((D, win_len), jnp.bfloat16),
            pltpu.VMEM((TAPS, D, D // 2), jnp.bfloat16),
            pltpu.VMEM((TAPS, D, D // 2), jnp.bfloat16),
            pltpu.SemaphoreType.DMA,
        ],
        win_len * TAPS * D * D,
        after,
    )(scalars, x, d_conv)


def input_gradient(scalars, d_conv, d_middle, gathered, block, after=()):
    win_len = d_conv.shape[0]
    arrays, others, places = gathered
    arrays = arrays + others
    return call(
        functools.partial(input_grad_kernel, SPACINGS[block], places),
        (1,),
        [whole(d_conv.shape), whole(d_conv.shape)] + [ANY] * len(arrays),
        whole(d_conv.shape),
        shape_of((win_len, D), jnp.bfloat16),
        [
            pltpu.VMEM((TAPS * D, D), jnp.bfloat16),
            padded_scratch(win_len, SPACINGS[block]),
            pltpu.SemaphoreType.DMA,
        ],
        win_len * TAPS * D * D,
        after,
    )(scalars, d_conv, d_middle, *arrays)


def schulz(parts, after=()):
    first, second = parts

    def body(*refs):
        schulz_kernel(refs[: len(first)], refs[len(first) : len(first) + len(second)], refs[-1])

    arrays = [*first, *second]
    return pl.pallas_call(
        body,
        in_specs=[whole(array.shape) for array in arrays] + [ANY] * len(after),
        out_specs=whole((D, D)),
        out_shape=shape_of((D, D), jnp.float32),
        compiler_params=params(LESS_BYTES),
        cost_estimate=cost(17 * 3 * D * D * D),
    )(*arrays, *after)


def plain(kernel, arrays, out_shapes, scratch=(), scalars=None):
    if scalars is not None:
        return call(
            kernel,
            (1,),
            [whole(array.shape) for array in arrays],
            [whole(shape) for shape in out_shapes],
            [shape_of(shape, jnp.bfloat16) for shape in out_shapes],
            list(scratch),
            1 << 20,
            limit=LESS_BYTES,
        )(scalars, *arrays)
    return pl.pallas_call(
        kernel,
        out_shape=[shape_of(shape, jnp.bfloat16) for shape in out_shapes],
        compiler_params=params(LESS_BYTES),
        cost_estimate=cost(1 << 20),
    )(*arrays)


def split_sums(terms, rows, bits, keys):
    arrays = [array for part in terms for array, _ in part]
    plan = [
        (bit, [first for _, first in part], part_keys)
        for bit, part, part_keys in zip(bits, terms, keys)
    ]
    count, wide = arrays[0].shape[0], arrays[0].shape[2]
    outs = plain(
        functools.partial(split_sums_kernel, plan), arrays, [(count // 2, rows, wide)] * 4
    )
    return outs[0::2], outs[1::2]


def add_cores(own, keep, got):
    groups, rows, wide = keep.shape
    relative = pl.BlockSpec((1, rows, wide), lambda step, s: (step, 0, 0))
    return call(
        add_cores_kernel,
        (groups,),
        [relative, relative],
        pl.BlockSpec((1, rows, wide), lambda step, s: (step ^ s[0], 0, 0)),
        shape_of(keep.shape, jnp.bfloat16),
        [],
        1 << 20,
        limit=LESS_BYTES,
    )(own.reshape(1).astype(jnp.int32), keep, got)


def last_sums(me, terms, rows, count):
    arrays = [array for part in terms for array, _ in part]
    wide = arrays[0].shape[2]
    return plain(
        functools.partial(last_sums_kernel, count),
        arrays,
        [(2 * rows // count, wide)] * count,
        [pltpu.VMEM((2 * rows, wide), jnp.float32)],
        me.reshape(1).astype(jnp.int32),
    )


def add_all(arrays):
    return plain(add_all_kernel, arrays, [arrays[0].shape])[0]


def join_parts(scalars, first, second):
    count = len(first)
    share, wide = first[0].shape
    return plain(
        functools.partial(join_parts_kernel, count),
        [*first, second],
        [(count * share, wide)] * 2,
        (),
        scalars,
    )


def packed_shapes():
    count = len(tiles_of(D)) // 2
    return [(count, LANES, LANES)] * 2


def conv_states(core, mine, got, moment, after=()):
    chunk = moment.shape[0]
    rows = chunk // 3
    shapes = packed_shapes()
    return call(
        conv_state_kernel,
        (3,),
        [tile(rows, D // 2), tile(rows, D // 2), tile(rows, D)],
        [tile(rows, D), tile(rows, D)] + [whole(shape) for shape in shapes],
        [shape_of((chunk, D), jnp.float32)] * 2
        + [shape_of(shape, jnp.float32) for shape in shapes],
        [pltpu.VMEM((D, D), jnp.float32)] * 2,
        2 * chunk * D * D,
        after,
        LESS_BYTES,
    )(core, mine, got, moment)


def pair_states(core, mine, got, up_moment, down_moment, after=()):
    shapes = packed_shapes() * 2
    outs = [up_moment.shape, down_moment.shape] * 2 + shapes
    return call(
        pair_state_kernel,
        (1,),
        [whole(value.shape) for value in (mine, got, up_moment, down_moment)],
        [whole(shape) for shape in outs],
        [shape_of(shape, jnp.float32) for shape in outs],
        [],
        4 * up_moment.shape[1] * D * D,
        after,
        LESS_BYTES,
    )(core, mine, got, up_moment, down_moment)


def on_device(
    inputs,
    cotangent,
    lengths,
    species,
    conv_weight,
    up_weight,
    down_weight,
    conv_moment,
    up_moment,
    down_moment,
    vec_values,
    vec_first,
    vec_second,
    head_weight,
    head_bias,
):
    core = lax.axis_index("section")
    own = lax.axis_index("ns")
    groups = lax.axis_size("ns")
    feature = inputs.shape[2]
    wide = FF // groups

    half = feature // 2

    def conv_half(side):
        return lax.dynamic_slice_in_dim(conv_weight[0], side * half, half, 1).astype(jnp.bfloat16)

    pair_low = jnp.stack(
        [up_weight[0].astype(jnp.bfloat16), down_weight[0].astype(jnp.bfloat16).T]
    )

    def pair_half(side):
        return lax.dynamic_slice_in_dim(pair_low, side * half, half, 1)

    leaving = together([conv_half(1 - core), pair_half(1 - core)])
    conv_got, pair_got = together([swap_cores(value) for value in leaving])
    conv_mine, pair_mine = conv_half(core), pair_half(core)
    conv_parts = [
        jnp.where(core == block, conv_mine, conv_got) for block in range(2)
    ]
    pair_parts = [
        jnp.where(core == block, pair_mine, pair_got) for block in range(2)
    ]
    conv_tasks = [Task(gather_rows(part, "ns")) for part in conv_parts]
    pairs = lax.all_gather(jnp.stack(pair_parts), "ns")
    vectors = in_order(core, vec_values[0], swap_cores(vec_values[0]))
    finish(conv_tasks[0])
    pairs = together([pairs], conv_tasks[0].result[1][-1])[0]

    batches = inputs.shape[0] // 2
    win_len = inputs.shape[1]
    species_range = jnp.arange(SPECIES)
    classes = head_weight.shape[1]
    head = jnp.pad(head_weight, ((0, 0), (0, LANES - classes)))
    head_shift = jnp.pad(head_bias[None], ((0, 0), (0, LANES - classes)), constant_values=-1e30)
    prob_sums = [jnp.zeros((SPECIES, classes), jnp.float32)] * 2
    token_counts = jnp.zeros((SPECIES,), jnp.float32)
    kept = {}
    outputs = [[], []]
    input_grads = [[], []]

    def add_up(name, values):
        kept[name] = values if name not in kept else [a + b for a, b in zip(kept[name], values)]

    def own_windows(parts):
        mine = jnp.stack(parts[0]), jnp.stack(parts[1])
        (got,) = yield [(jnp.where(core == 0, mine[1], mine[0]), swap_cores)]
        joined = in_order(core, jnp.where(core == 0, mine[0], mine[1]), got)
        return joined.reshape((1, 2 * batches) + joined.shape[2:])

    for batch in range(batches):
        window = core * batches + batch
        length = at(lengths, window)
        scalars = jnp.stack([length, own, core]).astype(jnp.int32)
        species_hit = (species_range == at(species, window)).astype(jnp.float32)
        token_counts = token_counts + species_hit * length.astype(jnp.float32)
        values = at(inputs, window)
        last = batch == batches - 1
        norms, inputs_of = [], []
        for block in range(2):
            x = values
            if batch == 0 and block == 1:
                finish(conv_tasks[1])
            conv = [task.result for task in conv_tasks]

            def convolve(after=()):
                return conv_forward(scalars, x, vectors[block], conv[block], block, after=after)

            def feed_forward(after=()):
                return pair_forward(
                    scalars,
                    middle,
                    vectors[block],
                    bias,
                    head,
                    head_shift,
                    (pairs, others),
                    block,
                    after=after,
                )

            bias = vectors[block][3:7].reshape(groups, wide)
            early = batch == 0 and block == 0
            n1, slope1, middle, low = run([conv_tasks[1]], convolve) if early else convolve()
            if early:
                pairs = together([pairs], low)[0]
                others = together([swap_cores(pairs)])[0]
            norms.append((n1, slope1))
            inputs_of.append(x)
            if block == 1:
                break
            n2, scale2, values, probs = (
                run([conv_tasks[1]], feed_forward) if early else feed_forward()
            )
            outputs[0].append(values)
            prob_sums[0] = prob_sums[0] + species_hit[:, None] * probs[:1, :classes]
            saved = low, n2, scale2
        grad = at(cotangent, window)
        last = batch == batches - 1
        for block in (1, 0):
            x = inputs_of[block]
            bias = vectors[block][3:7].reshape(groups, wide)
            if block == 1:
                first_saved, saved = saved, (middle, head, head_shift)
            else:
                saved = first_saved

            def inner(after):
                return inner_backward(
                    scalars,
                    grad,
                    norms[block],
                    vectors[block],
                    bias,
                    saved,
                    (pairs, others),
                    block,
                    block == 1,
                    after=after,
                )

            def outer(after):
                return conv_grad(
                    scalars, x, d_conv, d_middle, conv[block], block, groups, after=after
                )

            if last and block == 0:
                conv_one = Task(sum_cores(own, *kept["conv", 1]))
                pair_one = lax.psum_scatter(pair_one.result, "ns", scatter_dimension=0)
                made = run([conv_one, shared_out], inner)
            else:
                made = inner(())
            if block == 1:
                *made, values, probs = made
                outputs[1].append(values)
                prob_sums[1] = prob_sums[1] + species_hit[:, None] * probs[:1, :classes]
            d_middle, d_conv, sums, bias_sums, *pair_terms = made
            add_up(("pair", block), pair_terms)
            vec_sums = jnp.concatenate(
                [sums[0:3], bias_sums.reshape(-1, feature), sums[7:10]]
            )
            add_up(("vec", block), [vec_sums])
            if last and block == 1:
                pair_one = Task(sum_cores(own, *kept["pair", 1]))
                shared_out = Task(own_windows(outputs))
                *terms, grad = run([pair_one], outer)
            elif last:
                pair_zero = Task(reduce_groups(*kept["pair", 0]))
                *terms, grad = run([pair_zero], outer, also=[pair_one])
            else:
                *terms, grad = outer(pair_terms)
            add_up(("conv", block), terms)
            input_grads[block].append(grad)

    conv_zero = Task(reduce_groups(*kept["conv", 0]))
    conv_one = together([conv_one.result], pair_one)[0]
    conv_one = lax.psum_scatter(conv_one, "ns", scatter_dimension=0)

    def small_parts(block):
        tail = jnp.concatenate([prob_sums[block].reshape(-1), token_counts])
        tail = jnp.pad(tail, (0, feature - tail.size))
        return jnp.concatenate([kept["vec", block][0], tail[None]])

    mine, theirs = small_parts(0), small_parts(1)
    small = Task(
        sum_small(jnp.where(core == 0, mine, theirs), jnp.where(core == 0, theirs, mine))
    )
    shared_in = Task(own_windows(input_grads))
    run([conv_zero])
    run([conv_zero], also=[conv_one])
    conv_one, pair_one = together([conv_one, pair_one], conv_zero.wanted[0][0])
    conv_one, pair_one = lax.psum((conv_one, pair_one), "dp")
    run([conv_zero, pair_zero])
    run([conv_zero, pair_zero])
    run([conv_zero, pair_zero])
    finish(conv_zero, pair_zero)
    place = jnp.stack([lax.axis_index("dp"), core]).astype(jnp.int32)
    core_scalar = place[1:]
    conv_one, pair_one = together([conv_one, pair_one], conv_zero.result[0])
    conv_all = Task(own_block(*join_parts(place, conv_zero.result, conv_one)))
    run([conv_all, pair_zero, small])
    pair_all = Task(own_block(*join_parts(place, finish(pair_zero), pair_one)))
    conv_total, conv_state, *conv_gram = run(
        [pair_all, small],
        lambda after: conv_states(core_scalar, *conv_all.result, conv_moment[0], after),
    )
    conv_gram = Task(sum_both_ways(conv_gram, "ns"))
    up_grad, down_grad, up_state, down_state, *grams = run(
        [conv_gram, small],
        lambda after: pair_states(
            core_scalar, *pair_all.result, up_moment[0], down_moment[0], after
        ),
    )
    up_gram = Task(sum_both_ways(grams[:2], "ns"))
    down_gram = Task(sum_both_ways(grams[2:], "ns"))
    run([conv_gram, up_gram])
    gram = finish(conv_gram)
    (conv_turn,) = run([up_gram, down_gram, small], lambda after: [schulz(gram, after)])
    gram = finish(up_gram)
    (up_turn,) = run([down_gram, small], lambda after: [schulz(gram, after)])
    gram = finish(down_gram)
    (down_turn,) = run([shared_in, small], lambda after: [schulz(gram, after)])
    activations, input_grad, small = shared_out.result, shared_in.result, finish(small)
    vec_grad = small[:-1]
    prob_total = small[-1, : prob_sums[0].size].reshape(prob_sums[0].shape)
    count_total = small[-1, prob_sums[0].size : prob_sums[0].size + SPECIES]

    def product(left, right, contract):
        return lax.dot_general(
            left,
            right,
            (contract, ((), ())),
            precision=lax.Precision.HIGH,
            preferred_element_type=jnp.float32,
        )

    up_orth = product(up_turn, up_state, ((0,), (0,)))
    down_orth = product(down_state, down_turn, ((1,), (0,)))
    conv_orth = product(conv_state, conv_turn, ((1,), (0,)))
    keep_factor = 1.0 - MUON_RATE * MUON_DECAY
    conv_next = conv_weight[0] * keep_factor - MUON_RATE * 0.2 * math.sqrt(9 * D) * conv_orth
    up_next = up_weight[0] * keep_factor - MUON_RATE * 0.2 * math.sqrt(FF) * up_orth
    down_next = down_weight[0] * keep_factor - MUON_RATE * 0.2 * math.sqrt(FF) * down_orth
    first_next = BETA_ONE * vec_first[0] + (1.0 - BETA_ONE) * vec_grad
    second_next = BETA_TWO * vec_second[0] + (1.0 - BETA_TWO) * vec_grad * vec_grad
    vec_next = vec_values[0] * (1.0 - ADAM_RATE * ADAM_DECAY) - ADAM_RATE * (
        first_next / (1.0 - BETA_ONE**STEP)
    ) / (jnp.sqrt(second_next / (1.0 - BETA_TWO**STEP)) + ADAM_EPSILON)
    species_freq = prob_total / jnp.maximum(count_total, 1.0)[:, None]
    species_share = SPECIES * count_total / jnp.sum(count_total)
    return (
        activations,
        input_grad,
        conv_total[None],
        up_grad[None],
        down_grad[None],
        conv_state[None],
        up_state[None],
        down_state[None],
        conv_next[None],
        up_next[None],
        down_next[None],
        conv_next.astype(jnp.bfloat16)[None],
        up_next.astype(jnp.bfloat16)[None],
        down_next.astype(jnp.bfloat16)[None],
        vec_grad[None],
        first_next[None],
        second_next[None],
        vec_next[None],
        species_freq[None],
        species_share[None],
    )


def solution(mesh):
    placed = (
        P(("dp", "ns"), None, None),
        P(("dp", "ns"), None, None),
        P(("dp", "ns")),
        P(("dp", "ns")),
        P("section", "ns", None),
        P("section", None, "ns"),
        P("section", "ns", None),
        P("section", "ns", None),
        P("section", None, "ns"),
        P("section", "ns", None),
        P("section", None, None),
        P("section", None, None),
        P("section", None, None),
        P(),
        P(),
    )
    return jax.shard_map(
        on_device,
        mesh=mesh,
        in_specs=placed,
        out_specs=(
            P("section", ("dp", "ns"), None, None),
            P("section", ("dp", "ns"), None, None),
            P("section", "ns", None),
            P("section", None, "ns"),
            P("section", "ns", None),
            P("section", "ns", None),
            P("section", None, "ns"),
            P("section", "ns", None),
            P("section", "ns", None),
            P("section", None, "ns"),
            P("section", "ns", None),
            P("section", "ns", None),
            P("section", None, "ns"),
            P("section", "ns", None),
            P("section", None, None),
            P("section", None, None),
            P("section", None, None),
            P("section", None, None),
            P("section", None, None),
            P("section", None),
        ),
        check_vma=False,
    )
```
